512 devices in a mesh: grp: 16 (over z, core), sp: 32 (over x, y).
Axes of the slice: x: 4, y: 8, z: 8, core: 2. Of those that a mesh axis runs over, the one named last changes fastest.
Arguments:
- q_src: bfloat16 [128, 16, 32, 4096], P(None, 'grp', 'sp'), may hold values from -4.5 to 4.5
- k_src: bfloat16 [128, 16, 32, 1024], P(None, 'grp', 'sp'), may hold values from -4.5 to 4.5
- v_src: bfloat16 [128, 16, 32, 1024], P(None, 'grp', 'sp'), may hold values from -4.5 to 4.5
- grad_src: bfloat16 [128, 16, 32, 4096], P(None, 'grp', 'sp'), may hold values from -4.5 to 4.5
- doc_lengths: int32 [192], replicated, may hold values from 0 to 5, as said below
- doc_groups: int32 [192], replicated, may hold values from 0 to 15, as said below
- doc_offsets: int32 [192], replicated, may hold values from 0 to 11, as said below
Outputs:
- dq_grp: bfloat16 [16, 192, 32, 4096], P('grp', None, 'sp')
- dk_grp: bfloat16 [16, 192, 32, 1024], P('grp', None, 'sp')
- dv_grp: bfloat16 [16, 192, 32, 1024], P('grp', None, 'sp')
The draws below stay inside these ranges and needn't reach their ends.
Inputs may be any that keep to these rules, and one draw needn't show every extreme that they name: `doc_lengths`: documents of positive length come first, absent ones (length 0) last; the lengths sum to 128 and one document has exactly 5 blocks. `doc_groups`: placed at their offsets, the documents of a group cover its blocks 0 up to its total without gaps or intersection; every group receives at least one block, none more than 12, and one group exactly 12. Absent documents name group 0. `doc_offsets`: absent documents have offset 0.
All inputs are finite; a program needn't handle non-finite values.
Results may differ from the reference program's by a relative error of at most 0.0091.
Values may be sent and summed in bfloat16 or wider, within the bound.
No kernel may reach another device: no remote copies, remote signals or barrier semaphores. Data moves between devices by JAX's collectives and lax.ppermute only.
A program may use at most 64 MiB of HBM per device.

```python
import jax
import jax.numpy as jnp
from jax import lax

HEADS = 32
KV_HEADS = 8
HEAD_DIM = 128
TOK_DEV = 128
MAXDOC = 5
CAP = 12
UNIT = 512
GROUP_ROWS = 192
GROUP_TOK = 6144
N_GRP = 16
N_SP = 32


def draw_q_src(key, part):
    key = jax.random.fold_in(key, 12)
    full_shape = (TOK_DEV, N_GRP, N_SP, KV_HEADS, HEADS // KV_HEADS, HEAD_DIM)
    values = jnp.clip(jax.random.normal(key, full_shape, jnp.float32), -4.5, 4.5)
    return values.reshape(TOK_DEV, N_GRP, N_SP, HEADS * HEAD_DIM).astype(jnp.bfloat16)


def draw_k_src(key, part):
    key = jax.random.fold_in(key, 11)
    full_shape = (TOK_DEV, N_GRP, N_SP, KV_HEADS, HEAD_DIM)
    values = jnp.clip(jax.random.normal(key, full_shape, jnp.float32), -4.5, 4.5)
    return values.reshape(TOK_DEV, N_GRP, N_SP, KV_HEADS * HEAD_DIM).astype(jnp.bfloat16)


def plan_tables(key):
    key_move, key_amount, key_full, key_split, key_order = jax.random.split(key, 5)
    groups_idx = jnp.arange(N_GRP, dtype=jnp.int32)
    group_load = jnp.full((N_GRP,), TOK_DEV // N_GRP, jnp.int32) + (groups_idx < TOK_DEV % N_GRP).astype(jnp.int32)
    move_count = 4 * N_GRP
    move_pairs = jax.random.randint(key_move, (move_count, 2), 0, N_GRP)
    move_sizes = jax.random.randint(key_amount, (move_count,), 1, MAXDOC + 2)

    def shuffle_step(step_idx, group_load):
        to_group = move_pairs[step_idx, 0]
        from_group = move_pairs[step_idx, 1]
        amount = jnp.minimum(jnp.minimum(move_sizes[step_idx], CAP - group_load[to_group]), group_load[from_group] - 1)
        amount = jnp.where(to_group == from_group, 0, jnp.maximum(amount, 0))
        return group_load.at[to_group].add(amount).at[from_group].add(-amount)
    group_load = lax.fori_loop(0, move_count, shuffle_step, group_load)
    full_group = jax.random.randint(key_full, (), 0, N_GRP)

    def fill_step(group_id, carried):
        group_load, still_need = carried
        taken = jnp.where(group_id == full_group, 0, jnp.minimum(group_load[group_id] - 1, still_need))
        return (group_load.at[group_id].add(-taken), still_need - taken)
    group_load, still_need = lax.fori_loop(0, N_GRP, fill_step, (group_load, CAP - group_load[full_group]))
    group_load = group_load.at[full_group].set(CAP)
    unit_idx = jnp.arange(CAP, dtype=jnp.int32)
    new_flags = jax.random.randint(key_split, (N_GRP, CAP), 0, 2)
    is_full = (groups_idx == full_group)[:, None]
    new_flags = jnp.where(is_full & (unit_idx[None, :] >= 1) & (unit_idx[None, :] < MAXDOC), 0, new_flags)
    new_flags = jnp.where(is_full & (unit_idx[None, :] == CAP - 1), 1, new_flags)
    new_flags = new_flags.at[:, 0].set(1)

    def run_step(run_len, flag_col):
        begins = (flag_col == 1) | (run_len >= MAXDOC)
        return (jnp.where(begins, 1, run_len + 1), begins)
    unused, starts = lax.scan(run_step, jnp.full((N_GRP,), MAXDOC, jnp.int32), new_flags.T)
    starts = starts.T
    after_mask = (unit_idx[None, None, :] > unit_idx[None, :, None]) & starts[:, None, :]
    next_start = jnp.min(jnp.where(after_mask, unit_idx[None, None, :], CAP), axis=2)
    doc_ends = jnp.minimum(next_start, group_load[:, None])
    doc_real = starts & (unit_idx[None, :] < group_load[:, None])
    lengths = jnp.where(doc_real, doc_ends - unit_idx[None, :], 0).reshape(-1)
    sort_keys = jax.random.permutation(key_order, N_GRP * CAP).astype(jnp.int32) + N_GRP * CAP * (1 - doc_real.reshape(-1).astype(jnp.int32))
    pack_order = jnp.argsort(sort_keys)
    flat_len = lengths[pack_order].astype(jnp.int32)
    flat_grp = jnp.where(flat_len > 0, jnp.repeat(groups_idx, CAP)[pack_order], 0).astype(jnp.int32)
    flat_off = jnp.where(flat_len > 0, jnp.tile(unit_idx, N_GRP)[pack_order], 0).astype(jnp.int32)
    return (flat_len, flat_grp, flat_off)


def draw_doc_lengths(key, part):
    tables = plan_tables(key)
    return tables[0]


def draw_doc_groups(key, part):
    tables = plan_tables(key)
    return tables[1]


def draw_doc_offsets(key, part):
    tables = plan_tables(key)
    return tables[2]


def levels(rng, dims, shards, smallest, high):
    def one(dim, blocks):
        steps = jax.random.uniform(jax.random.fold_in(jax.random.fold_in(rng, 6), dim), (blocks,), jnp.float32, smallest / len(shards), high / len(shards))
        return jnp.repeat(jnp.exp(steps), dims[dim] // blocks).reshape((-1,) + (1,) * (len(dims) - dim - 1))

    gain = one(*shards[0])
    for cut in shards[1:]:
        gain = gain * one(*cut)
    return gain


def gaussian(key, dims, spread, bound, pieces=(), kind=jnp.bfloat16):
    values = spread * jax.random.normal(key, dims, jnp.float32)
    if pieces:
        values = values * levels(key, dims, pieces, -0.22, 0.18)
    return jnp.clip(values, -bound, bound).astype(kind)


def setup_inputs(seed: int = 0) -> dict:
    key_of = jax.random.split(jax.random.key(seed), 8)
    q_src = draw_q_src(jax.random.fold_in(key_of[7], 71), 0)
    k_src = draw_k_src(jax.random.fold_in(key_of[7], 71), 0)
    v_src = gaussian(key_of[2], (TOK_DEV, N_GRP, N_SP, KV_HEADS * HEAD_DIM), 1.0, 4.5, ((1, 16), (2, 32)))
    grad_src = gaussian(key_of[3], (TOK_DEV, N_GRP, N_SP, HEADS * HEAD_DIM), 1.0, 4.5, ((1, 16), (2, 32)))
    doc_lengths = draw_doc_lengths(jax.random.fold_in(key_of[7], 71), 0)
    doc_groups = draw_doc_groups(jax.random.fold_in(key_of[7], 71), 0)
    doc_offsets = draw_doc_offsets(jax.random.fold_in(key_of[7], 71), 0)
    return {"q_src": q_src, "k_src": k_src, "v_src": v_src, "grad_src": grad_src, "doc_lengths": doc_lengths, "doc_groups": doc_groups, "doc_offsets": doc_offsets}


NEG_FILL = -1.0e30


def unchanged(passed):
    return passed


def source_units(doc_lengths, doc_groups, doc_offsets):
    unit_ids = jnp.arange(TOK_DEV, dtype=jnp.int32)
    starts = (jnp.cumsum(doc_lengths) - doc_lengths).astype(jnp.int32)
    inside = ((unit_ids[:, None] >= starts[None, :]) & (unit_ids[:, None] < (starts + doc_lengths)[None, :])).astype(jnp.int32)
    group_of = jnp.sum(inside * doc_groups[None, :], axis=1).astype(jnp.int32)
    place_of = jnp.sum(inside * (doc_offsets[None, :] + unit_ids[:, None] - starts[None, :]), axis=1).astype(jnp.int32)
    slot_ids = jnp.arange(N_GRP * CAP, dtype=jnp.int32)
    matches = ((group_of * CAP + place_of)[None, :] == slot_ids[:, None]).astype(jnp.int32)
    source = jnp.sum(matches * unit_ids[None, :], axis=1).astype(jnp.int32).reshape(N_GRP, CAP)
    filled = (jnp.sum(matches, axis=1) > 0).reshape(N_GRP, CAP)
    return source, filled


def first_tokens(group_id, doc_lengths, doc_groups, doc_offsets):
    unit_place = jnp.arange(CAP, dtype=jnp.int32)
    member = ((doc_groups[None, :] == group_id) & (doc_lengths[None, :] > 0)
              & (doc_offsets[None, :] <= unit_place[:, None])
              & (unit_place[:, None] < (doc_offsets + doc_lengths)[None, :])).astype(jnp.int32)
    first_unit = jnp.sum(member * doc_offsets[None, :], axis=1).astype(jnp.int32)
    occupied = jnp.sum(member, axis=1) > 0
    token_ids = jnp.arange(GROUP_TOK, dtype=jnp.int32)
    return jnp.where(jnp.repeat(occupied, UNIT), jnp.repeat(first_unit * UNIT, UNIT), token_ids)


def attend_all(q_grp, k_grp, v_grp, g_grp, first_tok):
    span_len = UNIT
    blocks = CAP
    q_per_kv = HEADS // KV_HEADS
    factor = HEAD_DIM ** -0.5
    lane_pos = jnp.arange(span_len, dtype=jnp.int32)
    block_low = jnp.min(first_tok.reshape(blocks, span_len), axis=1)
    heads_shape = (KV_HEADS, q_per_kv, span_len)

    def cut_block(array, index):
        return lax.dynamic_slice_in_dim(array, (index * span_len).astype(jnp.int32), span_len, 0)

    def pair_logits(q_block, first_q, q_index, k_index):
        k_block = cut_block(k_grp, k_index).astype(jnp.float32)
        logits = jnp.einsum("qjih,kjh->jiqk", q_block, k_block) * factor
        q_pos = q_index * span_len + lane_pos
        k_pos = k_index * span_len + lane_pos
        allowed = (k_pos[None, :] <= q_pos[:, None]) & (k_pos[None, :] >= first_q[:, None])
        return logits, allowed

    def is_live(q_index, k_index):
        return block_low[q_index] <= k_index * span_len + span_len - 1

    def row_norm(q_index):
        q_block = cut_block(q_grp, q_index).astype(jnp.float32)
        first_q = cut_block(first_tok, q_index)

        def visit_key(k_index, running):
            def update(running):
                row_high, row_mass = running
                logits, allowed = pair_logits(q_block, first_q, q_index, k_index)
                logits = jnp.where(allowed, logits, NEG_FILL)
                new_high = jnp.maximum(row_high, jnp.max(logits, axis=-1))
                row_mass = row_mass * jnp.exp(row_high - new_high) + jnp.sum(
                    jnp.where(allowed, jnp.exp(logits - new_high[..., None]), 0.0), axis=-1)
                return new_high, row_mass
            return lax.cond(is_live(q_index, k_index), update, unchanged, running)

        initial = (jnp.full(heads_shape, NEG_FILL, jnp.float32), jnp.zeros(heads_shape, jnp.float32))
        row_high, row_mass = lax.fori_loop(0, q_index + 1, visit_key, initial)
        return row_high + jnp.log(row_mass)

    log_norm = lax.map(row_norm, jnp.arange(blocks, dtype=jnp.int32))

    def row_delta(q_index):
        q_block = cut_block(q_grp, q_index).astype(jnp.float32)
        first_q = cut_block(first_tok, q_index)
        norm_row = log_norm[q_index]

        def visit_key(k_index, acc_out):
            def update(acc_out):
                logits, allowed = pair_logits(q_block, first_q, q_index, k_index)
                weights = jnp.where(allowed, jnp.exp(logits - norm_row[..., None]), 0.0)
                weights = lax.optimization_barrier(weights.astype(jnp.bfloat16)).astype(jnp.float32)
                v_block = cut_block(v_grp, k_index).astype(jnp.float32)
                return acc_out + jnp.einsum("jiqk,kjh->jiqh", weights, v_block)
            return lax.cond(is_live(q_index, k_index), update, unchanged, acc_out)

        acc_out = lax.fori_loop(0, q_index + 1, visit_key, jnp.zeros(heads_shape + (HEAD_DIM,), jnp.float32))
        g_block = cut_block(g_grp, q_index).astype(jnp.float32)
        return jnp.einsum("jiqh,qjih->jiq", acc_out, g_block)

    delta_all = lax.map(row_delta, jnp.arange(blocks, dtype=jnp.int32))

    def back_row(q_index, carried):
        grad_q, grad_k, grad_v = carried
        q_block = cut_block(q_grp, q_index).astype(jnp.float32)
        g_block = cut_block(g_grp, q_index).astype(jnp.float32)
        first_q = cut_block(first_tok, q_index)
        norm_row = log_norm[q_index]
        delta_row = delta_all[q_index]

        def visit_key(k_index, inner):
            def update(inner):
                q_acc, grad_k, grad_v = inner
                logits, allowed = pair_logits(q_block, first_q, q_index, k_index)
                probs = jnp.where(allowed, jnp.exp(logits - norm_row[..., None]), 0.0)
                probs_low = lax.optimization_barrier(probs.astype(jnp.bfloat16)).astype(jnp.float32)
                k_block = cut_block(k_grp, k_index).astype(jnp.float32)
                v_block = cut_block(v_grp, k_index).astype(jnp.float32)
                d_probs = jnp.einsum("qjih,kjh->jiqk", g_block, v_block)
                d_logits = probs * (d_probs - delta_row[..., None])
                d_logits = lax.optimization_barrier(d_logits.astype(jnp.bfloat16)).astype(jnp.float32)
                q_acc = q_acc + jnp.einsum("jiqk,kjh->qjih", d_logits, k_block)
                k_part = jnp.einsum("jiqk,qjih->kjih", d_logits, q_block)
                v_part = jnp.einsum("jiqk,qjih->kjih", probs_low, g_block)
                at_row = (k_index * span_len).astype(jnp.int32)
                grad_k = lax.dynamic_update_slice_in_dim(grad_k, cut_block(grad_k, k_index) + k_part, at_row, 0)
                grad_v = lax.dynamic_update_slice_in_dim(grad_v, cut_block(grad_v, k_index) + v_part, at_row, 0)
                return q_acc, grad_k, grad_v
            return lax.cond(is_live(q_index, k_index), update, unchanged, inner)

        q_start = jnp.zeros((span_len, KV_HEADS, q_per_kv, HEAD_DIM), jnp.float32)
        q_acc, grad_k, grad_v = lax.fori_loop(0, q_index + 1, visit_key, (q_start, grad_k, grad_v))
        grad_q = lax.dynamic_update_slice_in_dim(grad_q, q_acc, (q_index * span_len).astype(jnp.int32), 0)
        return grad_q, grad_k, grad_v

    empty = jnp.zeros((GROUP_TOK, KV_HEADS, q_per_kv, HEAD_DIM), jnp.float32)
    grad_q, grad_k, grad_v = lax.fori_loop(0, blocks, back_row, (empty, empty, empty))
    return grad_q * factor, grad_k * factor, grad_v


def paired_total(grad_head):
    head_low = lax.optimization_barrier(grad_head.astype(jnp.bfloat16)).astype(jnp.float32)
    half = head_low.shape[2] // 2
    paired = head_low[:, :, :half] + head_low[:, :, half:]
    paired = lax.optimization_barrier(paired.astype(jnp.bfloat16)).astype(jnp.float32)
    return jnp.sum(paired, axis=2).astype(jnp.bfloat16)


def reference(q_src, k_src, v_src, grad_src, doc_lengths, doc_groups, doc_offsets):
    source, filled = source_units(doc_lengths, doc_groups, doc_offsets)
    q_per_kv = HEADS // KV_HEADS

    def one_group(group_id):
        picked = source[group_id]
        keep_mask = filled[group_id]

        def to_group(array, head_count):
            rows_now = jnp.take(array, picked, axis=0)
            rows_now = jnp.where(keep_mask[:, None, None, None], rows_now, jnp.zeros_like(rows_now))
            return rows_now.reshape(GROUP_TOK, head_count, HEAD_DIM)

        q_grp = to_group(q_src, HEADS).reshape(GROUP_TOK, KV_HEADS, q_per_kv, HEAD_DIM)
        g_grp = to_group(grad_src, HEADS).reshape(GROUP_TOK, KV_HEADS, q_per_kv, HEAD_DIM)
        k_grp = to_group(k_src, KV_HEADS)
        v_grp = to_group(v_src, KV_HEADS)
        first_tok = first_tokens(group_id, doc_lengths, doc_groups, doc_offsets)
        grad_q, grad_k, grad_v = attend_all(q_grp, k_grp, v_grp, g_grp, first_tok)
        out_q = grad_q.astype(jnp.bfloat16).reshape(GROUP_ROWS, N_SP, HEADS * HEAD_DIM)
        out_k = paired_total(grad_k).reshape(GROUP_ROWS, N_SP, KV_HEADS * HEAD_DIM)
        out_v = paired_total(grad_v).reshape(GROUP_ROWS, N_SP, KV_HEADS * HEAD_DIM)
        return out_q, out_k, out_v

    dq_all, dk_all, dv_all = lax.map(one_group, jnp.arange(N_GRP, dtype=jnp.int32))
    return (dq_all, dk_all, dv_all)
```

```python
import functools, math
import jax, jax.numpy as jnp
from jax import lax
from jax.experimental import pallas as pl
from jax.experimental.pallas import tpu as pltpu
from jax.sharding import Mesh, PartitionSpec as P

HEADS = 32
KV_HEADS = 8
HEAD_DIM = 128

CAPB=12
NT=(((1,),(1,)),((),()))
TN=(((0,),(0,)),((),()))
NN=(((1,),(0,)),((),()))
f32=jnp.float32; bf16=jnp.bfloat16

def dot(a,b,dims):
    return lax.dot_general(a,b,dims,preferred_element_type=f32)

def attn_kernel(first_ref, r_ref, kv_ref, dq_ref, dkv_ref, qg, s_scr, p_scr, dk_acc, dv_acc, dq_acc, *, WS, ngrp, nsp, hd):
    i=pl.program_id(0)
    cap=CAPB
    unit=ngrp*nsp
    c2=math.log2(math.e)/math.sqrt(hd)
    xs=kv_ref.shape[0]; tq=unit//xs
    rows=2*cap
    @pl.when(i==0)
    def _():
        n=ngrp*rows
        ri=lax.broadcasted_iota(jnp.int32,(n,n),0); ci=lax.broadcasted_iota(jnp.int32,(n,n),1)
        perm=jnp.where((ri//ngrp==ci%rows)&(ri%ngrp==ci//rows),1.0,0.0).astype(bf16)
        def one(s,_):
            blk=r_ref[:,s].reshape(n,hd)
            o=dot(perm,blk,NN).astype(bf16)
            qg[:,pl.ds(pl.multiple_of(s*ngrp,ngrp),ngrp),:]=o.reshape(rows,ngrp,hd)
            return 0
        lax.fori_loop(0,nsp,one,0)
    f=first_ref[i]
    at=pl.multiple_of(i*ngrp,ngrp)
    @pl.when(f<0)
    def _():
        z=jnp.zeros((nsp,ngrp,hd),bf16)
        dq_ref[:,pl.ds(at,ngrp),:]=z
        dkv_ref[:,pl.ds(at,ngrp),:]=z
        dkv_ref[:,pl.ds(pl.multiple_of(cap*ngrp+at,ngrp),ngrp),:]=z
    @pl.when(f>=0)
    def _():
        q=qg[i]; g=qg[cap+i]
        def kvb(row):
            return kv_ref[:,row].reshape(unit,hd)
        def pos(axis,base,shape):
            p=lax.broadcasted_iota(jnp.int32,shape,axis)+base
            return (p%ngrp)*nsp+p//ngrp
        def score(j,slot,st,masked):
            m,l,d=st
            kj=kvb(j); vj=kvb(cap+j)
            ss=[]
            mx=m
            for w in range(0,unit,WS):
                s=dot(kj[w:w+WS],q,NT)
                if masked:
                    s=jnp.where(pos(0,w,(WS,unit))<=pos(1,0,(WS,unit)),s,-1e30)
                s_scr[slot,w:w+WS,:]=s
                mx=jnp.maximum(mx,jnp.max(s,axis=0,keepdims=True))
            al=jnp.exp2((m-mx)*c2)
            l=l*al; d=d*al
            for w in range(0,unit,WS):
                dp=dot(vj[w:w+WS],g,NT)
                p_scr[slot,w:w+WS,:]=dp
                e=jnp.exp2((s_scr[slot,w:w+WS,:]-mx)*c2)
                l=l+jnp.sum(e,axis=0,keepdims=True)
                d=d+jnp.sum(e*dp,axis=0,keepdims=True)
            return mx,l,d
        st=(jnp.full((1,unit),-1e30,f32),jnp.zeros((1,unit),f32),jnp.zeros((1,unit),f32))
        st=score(i,i-f,st,True)
        st=lax.fori_loop(f,i,lambda j,s: score(j,j-f,s,False),st)
        m,l,d=st
        L=m*c2+jnp.log2(l)
        delta=d/l
        def back(j,slot,first):
            kj=kvb(j)
            acc=None
            for w in range(0,unit,WS):
                p=jnp.exp2(s_scr[slot,w:w+WS,:]*c2-L)
                ds=(p*(p_scr[slot,w:w+WS,:]-delta)).astype(bf16)
                dv=dot(p.astype(bf16),g,NN)
                dk=dot(ds,q,NN)
                t=dot(ds,kj[w:w+WS],TN)
                acc=t if acc is None else acc+t
                if first:
                    dv_acc[j,w:w+WS,:]=dv; dk_acc[j,w:w+WS,:]=dk
                else:
                    dv_acc[j,w:w+WS,:]+=dv; dk_acc[j,w:w+WS,:]+=dk
            if first: dq_acc[...]=acc
            else: dq_acc[...]+=acc
        back(i,i-f,True)
        def bl(j,_):
            back(j,j-f,False); return 0
        lax.fori_loop(f,i,bl,0)
        sc=1.0/math.sqrt(hd)
        dq_ref[:,pl.ds(at,ngrp),:]=(dq_acc[...]*sc).astype(bf16).reshape(nsp,ngrp,hd)
        nxt=jnp.where(i==cap-1,cap,first_ref[jnp.minimum(i+1,cap-1)])
        @pl.when(jnp.logical_or(nxt<0,nxt>i))
        def _():
            def put(j,_):
                aj=pl.multiple_of(j*ngrp,ngrp)
                dkv_ref[:,pl.ds(aj,ngrp),:]=(dk_acc[j]*sc).astype(bf16).reshape(nsp,ngrp,hd)
                dkv_ref[:,pl.ds(pl.multiple_of(cap*ngrp+aj,ngrp),ngrp),:]=dv_acc[j].astype(bf16).reshape(nsp,ngrp,hd)
                return 0
            lax.fori_loop(f,i+1,put,0)

def attention(first, r, kv, WS=128):
    ngrp,nsp,rows,hd=r.shape
    cap=rows//2; unit=ngrp*nsp
    full=lambda shape: pl.BlockSpec(shape, lambda i,*_: (0,)*len(shape))
    return pl.pallas_call(
        functools.partial(attn_kernel,WS=WS,ngrp=ngrp,nsp=nsp,hd=hd),
        out_shape=(jax.ShapeDtypeStruct((nsp,cap*ngrp,hd),bf16),jax.ShapeDtypeStruct((nsp,2*cap*ngrp,hd),bf16)),
        grid_spec=pltpu.PrefetchScalarGridSpec(
            num_scalar_prefetch=1, grid=(cap,),
            in_specs=[full(r.shape),full(kv.shape)],
            out_specs=(full((nsp,cap*ngrp,hd)),full((nsp,2*cap*ngrp,hd))),
            scratch_shapes=[pltpu.VMEM((rows,unit,hd),bf16),pltpu.VMEM((5,unit,unit),f32),pltpu.VMEM((5,unit,unit),f32),
                pltpu.VMEM((cap,unit,hd),f32),pltpu.VMEM((cap,unit,hd),f32),pltpu.VMEM((unit,hd),f32)]),
        compiler_params=pltpu.CompilerParams(vmem_limit_bytes=56*2**20,dimension_semantics=("arbitrary",)),
        name="attention",
    )(first,r,kv)


def pack_kernel(want_ref, a_ref, b_ref, out_ref):
    rows = want_ref.shape[0]
    units = a_ref.shape[0]
    groups, wide, _, per, width = out_ref.shape
    both = jnp.concatenate([a_ref[...], b_ref[...]], axis=0)
    column = lax.broadcasted_iota(jnp.int32, (rows, 2 * units), 1)
    pick = jnp.where(column == want_ref[...], 1.0, 0.0).astype(bf16)
    moved = dot(pick, both, NN).astype(bf16)
    for x in range(wide):
        out_ref[:, x, 0] = moved[:, x * width:(x + 1) * width].reshape(groups, per, width)


def pack(want, a, b, groups, wide):
    units, columns = a.shape
    rows = want.shape[0]
    steps = columns // (wide * HEAD_DIM)
    step_in = pl.BlockSpec((units, wide * HEAD_DIM), lambda y: (0, y))
    return pl.pallas_call(
        pack_kernel,
        out_shape=jax.ShapeDtypeStruct((groups, wide, steps, rows // groups, HEAD_DIM), bf16),
        grid=(steps,),
        in_specs=[pl.BlockSpec((rows, 1), lambda y: (0, 0)), step_in, step_in],
        out_specs=pl.BlockSpec((groups, wide, 1, rows // groups, HEAD_DIM), lambda y: (0, 0, y, 0, 0)),
        compiler_params=pltpu.CompilerParams(vmem_limit_bytes=32 * 2**20),
        name="pack",
    )(want, a, b)


def plan(doc_lengths, doc_groups, doc_offsets, units, groups, cap):
    starts = jnp.cumsum(doc_lengths) - doc_lengths
    place = jnp.arange(groups * cap, dtype=jnp.int32)
    low = doc_groups * cap + doc_offsets
    inside = (place[:, None] >= low[None, :]) & (place[:, None] < (low + doc_lengths)[None, :])
    source = jnp.sum(jnp.where(inside, (starts - low)[None, :] + place[:, None] + 1, 0), axis=1) - 1
    first = jnp.sum(jnp.where(inside, doc_offsets[None, :] + 1, 0), axis=1) - 1
    return source.reshape(groups, cap), first.reshape(groups, cap)


def on_device(q_src, k_src, v_src, grad_src, doc_lengths, doc_groups, doc_offsets):
    groups, n_x, n_y = lax.axis_size("grp"), lax.axis_size("x"), lax.axis_size("y")
    n_sp = n_x * n_y
    units = q_src.shape[0]
    cap = doc_lengths.shape[0] // groups
    source, first = plan(doc_lengths, doc_groups, doc_offsets, units, groups, cap)
    first_mine = lax.dynamic_index_in_dim(first, lax.axis_index("grp"), 0, keepdims=False)
    want = jnp.concatenate([source, jnp.where(source >= 0, source + units, -1)], axis=1).reshape(-1, 1)

    flat = lambda array: array.reshape(units, array.shape[-1])
    kv_out = pack(want, flat(k_src), flat(v_src), groups, 1)
    qg_out = pack(want, flat(q_src), flat(grad_src), groups, n_x)

    kv_in = lax.all_to_all(kv_out.reshape(groups * n_y, 2 * cap, HEAD_DIM), ("grp", "y"), 0, 0, tiled=True)
    kv_in = kv_in.reshape(groups, n_y, 2 * cap, HEAD_DIM).transpose(2, 1, 0, 3)
    kv_all = lax.all_gather(kv_in.reshape(2 * cap, n_y * groups, HEAD_DIM), "x", axis=0)
    qg_in = lax.all_to_all(qg_out.reshape(groups * n_sp, 2 * cap, HEAD_DIM), ("grp", "x", "y"), 0, 0, tiled=True)
    dq, dkv = attention(first_mine, qg_in.reshape(groups, n_sp, 2 * cap, HEAD_DIM), kv_all)

    dq_home = lax.all_to_all(dq, ("x", "y"), 0, 0, tiled=True)
    dkv_sum = lax.psum_scatter(dkv.reshape(n_x, n_y, 2 * cap * groups, HEAD_DIM), "x", scatter_dimension=0)
    dkv_home = lax.all_to_all(dkv_sum, "y", 0, 0, tiled=True)
    rows = cap * groups
    dq_out = dq_home.reshape(n_x, n_y, rows, HEAD_DIM).transpose(2, 1, 0, 3).reshape(1, rows, 1, HEADS * HEAD_DIM)
    dk_out = dkv_home[:, :rows].transpose(1, 0, 2).reshape(1, rows, 1, KV_HEADS * HEAD_DIM)
    dv_out = dkv_home[:, rows:].transpose(1, 0, 2).reshape(1, rows, 1, KV_HEADS * HEAD_DIM)
    return dq_out, dk_out, dv_out


def solution(mesh):
    groups = mesh.shape["grp"]
    split = Mesh(mesh.devices.reshape(groups, HEADS // KV_HEADS, KV_HEADS), ("grp", "x", "y"))
    placed = P(None, "grp", ("x", "y"), None)
    out = P("grp", None, ("x", "y"), None)
    return jax.shard_map(
        on_device,
        mesh=split,
        in_specs=(placed,) * 4 + (P(),) * 3,
        out_specs=(out,) * 3,
        check_vma=False,
    )
```

```python
import functools
import math

import jax
import jax.numpy as jnp
from jax import lax
from jax.experimental import pallas as pl
from jax.experimental.pallas import tpu as pltpu
from jax.sharding import Mesh, PartitionSpec as P

HEADS = 32
KV_HEADS = 8
HEAD_DIM = 128
MAXDOC = 5
EARLY = 4
NN = (((1,), (0,)), ((), ()))
NT = (((1,), (1,)), ((), ()))
TN = (((0,), (0,)), ((), ()))
f32 = jnp.float32
bf16 = jnp.bfloat16
NEG_FILL = -1e30


def dot(a, b, dims):
    return lax.dot_general(a, b, dims, preferred_element_type=f32)


def attention_kernel(begin, count, cap, n_x, has_carry, dqt, *refs):
    first_ref, where_ref, in_ref = refs[:3]
    k_refs, v_refs = refs[3:3 + n_x], refs[3 + n_x:3 + 2 * n_x]
    refs = refs[3 + 2 * n_x:]
    if has_carry:
        k_carry, v_carry, dq_ref = refs[:3]
        dk_refs, dv_refs = refs[3:3 + n_x], refs[3 + n_x:3 + 2 * n_x]
        queries, s_keep, p_keep, k_acc, v_acc, q_acc = refs[3 + 2 * n_x:]
    else:
        dq_ref, k_acc, v_acc, queries, s_keep, p_keep, q_acc = refs
    groups, n_y, rows, head_dim = in_ref.shape
    heads = n_x
    part = groups * n_y
    span = heads * part
    per = 2 * count
    factor = 1.0 / math.sqrt(head_dim)
    power = math.log2(math.e) * factor
    my_x = where_ref[0]

    mixed = groups * per
    row = lax.broadcasted_iota(jnp.int32, (mixed, mixed), 0)
    col = lax.broadcasted_iota(jnp.int32, (mixed, mixed), 1)
    turn = jnp.where((row // groups == col % per) & (row % groups == col // per), 1.0, 0.0).astype(bf16)

    def sort_y(y, _):
        taken = jnp.concatenate(
            [in_ref[:, y, h * per:(h + 1) * per, :].reshape(mixed, head_dim) for h in range(heads)], axis=1)
        turned = dot(turn, taken, NN).astype(bf16)
        for h in range(heads):
            at = pl.multiple_of(h * part + y * groups, groups)
            queries[:, pl.ds(at, groups), :] = (
                turned[:, h * head_dim:(h + 1) * head_dim].reshape(per, groups, head_dim))
        return 0

    lax.fori_loop(0, n_y, sort_y, 0)

    def put(block):
        at = pl.multiple_of(block * groups, groups)
        for x in range(n_x):
            dk_refs[x][:, pl.ds(at, groups), :] = (k_acc[x, block] * factor).astype(bf16).reshape(n_y, groups, head_dim)
            dv_refs[x][:, pl.ds(at, groups), :] = v_acc[x, block].astype(bf16).reshape(n_y, groups, head_dim)

    if has_carry:
        k_acc[:, :begin] = k_carry[...]
        v_acc[:, :begin] = v_carry[...]
        low = first_ref[begin]
        low = jnp.where(low < 0, begin, jnp.minimum(low, begin))
        lax.fori_loop(0, low, lambda block, _: (put(block), 0)[1], 0)

    key_row = lax.broadcasted_iota(jnp.int32, (part, span), 0)
    query_col = lax.broadcasted_iota(jnp.int32, (part, span), 1) % part
    key_pos = (key_row % groups) * (n_x * n_y) + key_row // groups
    query_pos = (query_col % groups) * (n_x * n_y) + query_col // groups + my_x * n_y

    def one_block(block, _):
        low = first_ref[block]
        local = block - begin
        at = pl.multiple_of(local * groups, groups)

        @pl.when(low < 0)
        def _():
            dq_ref[:, pl.ds(at, groups), :] = jnp.zeros((n_y, groups, heads * head_dim), bf16)
            zero = jnp.zeros((part, head_dim), f32)
            for x in range(n_x):
                k_acc[x, block] = zero
                v_acc[x, block] = zero
            if has_carry:
                put(block)

        @pl.when(low >= 0)
        def _():
            q = queries[local]
            g = queries[count + local]

            def score(key, stats, masked):
                high, mass, mean = stats
                slot = key - low
                top = high
                for x in range(n_x):
                    s = dot(k_refs[x][key], q, NT)
                    if masked:
                        x_of = lax.rem(my_x + x, n_x) * n_y
                        s = jnp.where(key_pos + x_of <= query_pos, s, NEG_FILL)
                    s_keep[slot, x] = s
                    top = jnp.maximum(top, jnp.max(s, axis=0, keepdims=True))
                shrink = jnp.exp2((high - top) * power)
                mass = mass * shrink
                mean = mean * shrink
                for x in range(n_x):
                    dp = dot(v_refs[x][key], g, NT)
                    p_keep[slot, x] = dp
                    e = jnp.exp2((s_keep[slot, x] - top) * power)
                    mass = mass + jnp.sum(e, axis=0, keepdims=True)
                    mean = mean + jnp.sum(e * dp, axis=0, keepdims=True)
                return top, mass, mean

            none = jnp.zeros((1, span), f32)
            stats = score(block, (none + NEG_FILL, none, none), True)
            stats = lax.fori_loop(low, block, lambda key, stats: score(key, stats, False), stats)
            high, mass, mean = stats
            norm = high * power + jnp.log2(mass)
            delta = mean / mass

            def back(key, fresh):
                slot = key - low
                total = None
                for x in range(n_x):
                    p = jnp.exp2(s_keep[slot, x] * power - norm)
                    ds = (p * (p_keep[slot, x] - delta)).astype(bf16)
                    dv = dot(p.astype(bf16), g, NN)
                    dk = dot(ds, q, NN)
                    if dqt:
                        dq = dot(k_refs[x][key], ds, TN)
                    else:
                        dq = dot(ds, k_refs[x][key], TN)
                    total = dq if total is None else total + dq
                    if fresh:
                        v_acc[x, key] = dv
                        k_acc[x, key] = dk
                    else:
                        v_acc[x, key] += dv
                        k_acc[x, key] += dk
                if fresh:
                    q_acc[...] = total
                else:
                    q_acc[...] += total

            back(block, True)
            lax.fori_loop(low, block, lambda key, _: (back(key, False), 0)[1], 0)
            for h in range(heads):
                if dqt:
                    mine = (q_acc[:, h * part:(h + 1) * part] * factor).T.astype(bf16)
                else:
                    mine = (q_acc[h * part:(h + 1) * part, :] * factor).astype(bf16)
                dq_ref[:, pl.ds(at, groups), h * head_dim:(h + 1) * head_dim] = mine.reshape(n_y, groups, head_dim)

            if has_carry:
                after = first_ref[jnp.minimum(block + 1, cap - 1)]

                @pl.when((block == cap - 1) | (after < 0) | (after > block))
                def _():
                    lax.fori_loop(low, block + 1, lambda key, _: (put(key), 0)[1], 0)
        return 0

    lax.fori_loop(begin, begin + count, one_block, 0)


def attention(first, my_x, packed, keys, values, begin, count, carry=None, dqt=False):
    groups, n_y, rows, head_dim = packed.shape
    n_x = len(keys)
    cap = first.shape[0]
    part = groups * n_y
    span = n_x * part
    vmem = pl.BlockSpec(memory_space=pltpu.VMEM)
    smem = pl.BlockSpec(memory_space=pltpu.SMEM)
    shape = jax.ShapeDtypeStruct
    dq = shape((n_y, count * groups, n_x * head_dim), bf16)
    slots = MAXDOC if carry is not None else min(MAXDOC, count)
    scratch = [
        pltpu.VMEM((2 * count, span, head_dim), bf16),
        pltpu.VMEM((slots, n_x, part, span), f32),
        pltpu.VMEM((slots, n_x, part, span), f32),
    ]
    sums = (n_x, begin + count, part, head_dim)
    total = [pltpu.VMEM((head_dim, span) if dqt else (span, head_dim), f32)]
    if carry is None:
        out = (dq, shape(sums, f32), shape(sums, f32))
        carry = ()
        scratch = scratch + total
    else:
        out = (dq,) + (shape((n_y, cap * groups, head_dim), bf16),) * (2 * n_x)
        scratch = scratch + [pltpu.VMEM(sums, f32)] * 2 + total
    pairs = count * 2
    return pl.pallas_call(
        functools.partial(attention_kernel, begin, count, cap, n_x, bool(carry), dqt),
        out_shape=out,
        in_specs=[smem, smem] + [vmem] * (1 + 2 * n_x + len(carry)),
        out_specs=(vmem,) * len(out),
        scratch_shapes=scratch,
        compiler_params=pltpu.CompilerParams(vmem_limit_bytes=48 * 2**20),
        cost_estimate=pl.CostEstimate(
            flops=pairs * 10 * span * span * head_dim, bytes_accessed=8 * 2**20, transcendentals=pairs * 2 * span * span),
        name="attention",
    )(first, my_x, packed, *keys, *values, *carry)


def pack_kernel(begin, count, cap, with_kv, *refs):
    lens_ref, groups_ref, offsets_ref, q_ref, g_ref = refs[:5]
    if with_kv:
        k_ref, v_ref, out_ref, pick, pick_kv = refs[5:]
    else:
        out_ref, pick = refs[5:]
    n_grp = out_ref.shape[0]
    units = q_ref.shape[0]
    head_dim = out_ref.shape[3]
    per = 2 * count

    @pl.when(pl.program_id(0) == 0)
    def _():
        lens = lens_ref[...]
        docs = lens.shape[1]
        before = lax.broadcasted_iota(jnp.int32, (docs, docs), 0) < lax.broadcasted_iota(jnp.int32, (docs, docs), 1)
        many = jnp.broadcast_to(lens, (16, docs)).astype(f32).astype(bf16)
        start = dot(many, jnp.where(before, 1.0, 0.0).astype(bf16), NN)[:1].astype(jnp.int32)
        low = groups_ref[...] * cap + offsets_ref[...]

        def choose(first, blocks, into):
            rows = n_grp * 2 * blocks
            row = lax.broadcasted_iota(jnp.int32, (rows, docs), 0)
            place = row // (2 * blocks) * cap + first + row % blocks
            inside = (place >= low) & (place < low + lens)
            source = jnp.sum(jnp.where(inside, start - low + place + 1, 0), axis=1, keepdims=True) - 1
            kind = lax.broadcasted_iota(jnp.int32, (rows, 1), 0) // blocks % 2
            wanted = jnp.where(source >= 0, source + kind * units, -1)
            column = lax.broadcasted_iota(jnp.int32, (rows, 2 * units), 1)
            into[...] = jnp.where(column == wanted, 1.0, 0.0).astype(bf16)

        choose(begin, count, pick)
        if with_kv:
            choose(0, cap, pick_kv)

    moved = dot(pick[...], jnp.concatenate([q_ref[...], g_ref[...]], axis=0), NN)
    heads = moved.shape[1] // head_dim
    for h in range(heads):
        slab = moved[:, h * head_dim:(h + 1) * head_dim].reshape(n_grp, per, head_dim)
        out_ref[:, 0, h * per:(h + 1) * per, :] = slab.astype(bf16)
    if with_kv:
        both = dot(pick_kv[...], jnp.concatenate([k_ref[...], v_ref[...]], axis=0), NN)
        out_ref[:, 0, heads * per:, :] = both.reshape(n_grp, 2 * cap, head_dim).astype(bf16)


def pack(tables, q, g, kv, n_grp, n_y, begin, count, cap):
    units = q.shape[0]
    heads = q.shape[1] // (n_y * HEAD_DIM)
    rows = heads * 2 * count + (2 * cap if kv else 0)
    table = pl.BlockSpec((1, tables[0].shape[1]), lambda y: (0, 0))
    wide = pl.BlockSpec((units, heads * HEAD_DIM), lambda y: (0, y))
    thin = pl.BlockSpec((units, HEAD_DIM), lambda y: (0, y))
    scratch = [pltpu.VMEM((n_grp * 2 * count, 2 * units), bf16)]
    if kv:
        scratch.append(pltpu.VMEM((n_grp * 2 * cap, 2 * units), bf16))
    return pl.pallas_call(
        functools.partial(pack_kernel, begin, count, cap, bool(kv)),
        out_shape=jax.ShapeDtypeStruct((n_grp, n_y, rows, HEAD_DIM), bf16),
        grid=(n_y,),
        in_specs=[table] * 3 + [wide] * 2 + [thin] * len(kv),
        out_specs=pl.BlockSpec((n_grp, 1, rows, HEAD_DIM), lambda y: (0, y, 0, 0)),
        scratch_shapes=scratch,
        compiler_params=pltpu.CompilerParams(vmem_limit_bytes=24 * 2**20),
        cost_estimate=pl.CostEstimate(flops=2 * 10**9, bytes_accessed=6 * 2**20, transcendentals=0),
        name="pack",
    )(*tables, q, g, *kv)


def add_kernel(*refs):
    out_ref = refs[-1]
    rows = out_ref.shape[1] // 2
    for half in range(2):
        a, b, c = refs[3 * half:3 * half + 3]
        total = a[...].astype(f32) + b[...].astype(f32) + c[...].astype(f32)
        out_ref[:, half * rows:(half + 1) * rows, :] = total.astype(bf16)


def add_up(dk_parts, dv_parts):
    n_y, rows, head_dim = dk_parts[0].shape
    vmem = pl.BlockSpec(memory_space=pltpu.VMEM)
    return pl.pallas_call(
        add_kernel,
        out_shape=jax.ShapeDtypeStruct((n_y, 2 * rows, head_dim), bf16),
        in_specs=[vmem] * 6,
        out_specs=vmem,
        compiler_params=pltpu.CompilerParams(vmem_limit_bytes=16 * 2**20),
        name="add_up",
    )(*dk_parts, *dv_parts)


def lay_kernel(pieces, *refs):
    sources = 1 + max(piece[0] for piece in pieces)
    for source, row, rows, target, at in pieces:
        taken, out_ref = refs[source], refs[sources + target]
        n_y, _, width = taken.shape
        for y in range(n_y):
            out_ref[at:at + rows, y * width:(y + 1) * width] = taken[y, row:row + rows, :]


def lay_out(arrays, pieces, shapes):
    vmem = pl.BlockSpec(memory_space=pltpu.VMEM)
    return pl.pallas_call(
        functools.partial(lay_kernel, pieces),
        out_shape=tuple(jax.ShapeDtypeStruct(shape, bf16) for shape in shapes),
        in_specs=[vmem] * len(arrays),
        out_specs=(vmem,) * len(shapes),
        compiler_params=pltpu.CompilerParams(vmem_limit_bytes=16 * 2**20),
        name="lay_out",
    )(*arrays)


def first_blocks(doc_lengths, doc_groups, doc_offsets, cap):
    place = jnp.arange(cap, dtype=jnp.int32)[:, None]
    here = (doc_groups == lax.axis_index("grp"))[None, :]
    member = here & (doc_offsets[None, :] <= place) & (place < (doc_offsets + doc_lengths)[None, :])
    return jnp.sum(jnp.where(member, doc_offsets[None, :] + 1, 0), axis=1) - 1


def step(array, by):
    n_x = lax.axis_size("x")
    return lax.ppermute(array, "x", [(i, (i + by) % n_x) for i in range(n_x)])


def on_device(q_src, k_src, v_src, grad_src, doc_lengths, doc_groups, doc_offsets):
    n_grp, n_x, n_y = lax.axis_size("grp"), lax.axis_size("x"), lax.axis_size("y")
    units = q_src.shape[0]
    docs = doc_lengths.shape[0]
    cap = docs // n_grp
    split = EARLY
    tables = tuple(table.reshape(1, docs) for table in (doc_lengths, doc_groups, doc_offsets))
    q, k, v, g = (array.reshape(units, array.shape[-1]) for array in (q_src, k_src, v_src, grad_src))

    def exchange(message):
        rows = message.shape[2]
        home = lax.all_to_all(message.reshape(n_grp * n_y, rows, HEAD_DIM), ("grp", "y"), 0, 0, tiled=True)
        return home.reshape(n_grp, n_y, rows, HEAD_DIM)

    early = exchange(pack(tables, q, g, (k, v), n_grp, n_y, 0, split, cap))
    late = exchange(pack(tables, q, g, (), n_grp, n_y, split, cap - split, cap))

    at = n_x * 2 * split
    k0, v0 = (
        early[:, :, at + i * cap:at + (i + 1) * cap].transpose(2, 1, 0, 3).reshape(cap, n_y * n_grp, HEAD_DIM)
        for i in range(2)
    )
    k3, v1 = step(k0, 1), step(v0, -1)
    v3, k1 = step(v0, 1), step(k0, -1)
    k2, v2 = step(k3, 1), step(v1, -1)
    keys, values = (k0, k1, k2, k3), (v0, v1, v2, v3)

    first = first_blocks(doc_lengths, doc_groups, doc_offsets, cap)
    my_x = lax.axis_index("x").astype(jnp.int32).reshape(1)
    dq_early, k_sums, v_sums = attention(first, my_x, early, keys, values, 0, split)
    dq_late, *grads = attention(first, my_x, late, keys, values, split, cap - split, (k_sums, v_sums))
    dk, dv = grads[:n_x], grads[n_x:]

    dq_early = lax.all_to_all(dq_early, "y", 0, 0, tiled=True)
    dq_late = lax.all_to_all(dq_late, "y", 0, 0, tiled=True)

    def joined(mine, came):
        return (mine.astype(f32) + came.astype(f32)).astype(bf16)

    k_far, v_far = step(dk[2], 1), step(dv[2], -1)
    v_up, k_down = step(dv[1], 1), step(dk[3], -1)
    k_up, v_down = step(joined(dk[1], k_far), 1), step(joined(dv[3], v_far), -1)
    sums = add_up((dk[0], k_up, k_down), (dv[0], v_up, v_down))
    sums = lax.all_to_all(sums, "y", 0, 0, tiled=True)

    rows, near = cap * n_grp, split * n_grp
    (dq_out,) = lay_out(
        (dq_early, dq_late), ((0, 0, near, 0, 0), (1, 0, rows - near, 0, near)), ((rows, HEADS * HEAD_DIM),))
    dk_out, dv_out = lay_out((sums,), ((0, 0, rows, 0, 0), (0, rows, rows, 1, 0)), ((rows, KV_HEADS * HEAD_DIM),) * 2)
    return tuple(array.reshape(1, rows, 1, array.shape[-1]) for array in (dq_out, dk_out, dv_out))


def solution(mesh):
    groups = mesh.shape["grp"]
    split = Mesh(mesh.devices.reshape(groups, HEADS // KV_HEADS, KV_HEADS), ("grp", "x", "y"))
    placed = P(None, "grp", ("x", "y"), None)
    out = P("grp", None, ("x", "y"), None)
    return jax.shard_map(
        on_device,
        mesh=split,
        in_specs=(placed,) * 4 + (P(),) * 3,
        out_specs=(out,) * 3,
        check_vma=False,
    )
```

```python
import functools
import math

import jax
import jax.numpy as jnp
from jax import lax
from jax.experimental import pallas as pl
from jax.experimental.pallas import tpu as pltpu
from jax.sharding import Mesh, PartitionSpec as P

HEADS = 32
KV_HEADS = 8
HEAD_DIM = 128
MAXDOC = 5
EARLY = 4
LIMIT = 60
NN = (((1,), (0,)), ((), ()))
NT = (((1,), (1,)), ((), ()))
TN = (((0,), (0,)), ((), ()))
f32 = jnp.float32
bf16 = jnp.bfloat16
NEG_FILL = -1e30


def dot(a, b, dims):
    return lax.dot_general(a, b, dims, preferred_element_type=f32)


def attention_kernel(begin, count, cap, n_x, has_carry, *refs):
    first_ref, where_ref, in_ref, own, right, left, far_k, far_v = refs[:8]
    k_from = ((own, 0), (right, 0), (far_k, 0), (left, 0))
    v_from = ((own, cap), (right, cap), (far_v, 0), (left, cap))
    if has_carry:
        k_carry, v_carry, dq_ref, out_own, out_up, out_down, out_k, out_v = refs[8:16]
        queries, s_keep, p_keep, k_acc, v_acc, q_acc = refs[16:]
    else:
        dq_ref, k_acc, v_acc, queries, s_keep, p_keep, q_acc = refs[8:]
    groups, n_y, rows, head_dim = in_ref.shape
    heads = n_x
    part = groups * n_y
    span = heads * part
    per = 2 * count
    factor = 1.0 / math.sqrt(head_dim)
    power = math.log2(math.e) * factor
    my_x = where_ref[0]

    def key_part(x, block):
        source, row = k_from[x]
        return source[row + block]

    def value_part(x, block):
        source, row = v_from[x]
        return source[row + block]

    mixed = groups * per
    row = lax.broadcasted_iota(jnp.int32, (mixed, mixed), 0)
    col = lax.broadcasted_iota(jnp.int32, (mixed, mixed), 1)
    turn = jnp.where((row // groups == col % per) & (row % groups == col // per), 1.0, 0.0).astype(bf16)

    def sort_y(y, _):
        taken = jnp.concatenate(
            [in_ref[:, y, h * per:(h + 1) * per, :].reshape(mixed, head_dim) for h in range(heads)], axis=1)
        turned = dot(turn, taken, NN).astype(bf16)
        for h in range(heads):
            at = pl.multiple_of(h * part + y * groups, groups)
            queries[:, pl.ds(at, groups), :] = (
                turned[:, h * head_dim:(h + 1) * head_dim].reshape(per, groups, head_dim))
        return 0

    lax.fori_loop(0, n_y, sort_y, 0)

    def put(block):
        at = pl.multiple_of(block * groups, groups)
        second = pl.multiple_of(at + cap * groups, groups)
        k_to = ((out_own, at), (out_k, at), (out_up, at), (out_down, at))
        v_to = ((out_own, second), (out_up, second), (out_down, second), (out_v, at))
        for x in range(n_x):
            target, row = k_to[x]
            target[:, pl.ds(row, groups), :] = (k_acc[x, block] * factor).astype(bf16).reshape(n_y, groups, head_dim)
            target, row = v_to[x]
            target[:, pl.ds(row, groups), :] = v_acc[x, block].astype(bf16).reshape(n_y, groups, head_dim)

    if has_carry:
        k_acc[:, :begin] = k_carry[...]
        v_acc[:, :begin] = v_carry[...]
        low = first_ref[begin]
        low = jnp.where(low < 0, begin, jnp.minimum(low, begin))
        lax.fori_loop(0, low, lambda block, _: (put(block), 0)[1], 0)

    key_row = lax.broadcasted_iota(jnp.int32, (part, span), 0)
    query_col = lax.broadcasted_iota(jnp.int32, (part, span), 1) % part
    key_pos = (key_row % groups) * (n_x * n_y) + key_row // groups
    query_pos = (query_col % groups) * (n_x * n_y) + query_col // groups + my_x * n_y

    def one_block(block, _):
        low = first_ref[block]
        local = block - begin
        at = pl.multiple_of(local * groups, groups)

        @pl.when(low < 0)
        def _():
            dq_ref[:, pl.ds(at, groups), :] = jnp.zeros((n_y, groups, heads * head_dim), bf16)
            zero = jnp.zeros((part, head_dim), f32)
            for x in range(n_x):
                k_acc[x, block] = zero
                v_acc[x, block] = zero
            if has_carry:
                put(block)

        @pl.when(low >= 0)
        def _():
            q = queries[local]
            g = queries[count + local]

            def score(key, stats, masked):
                high, mass, mean = stats
                slot = key - low
                top = high
                for x in range(n_x):
                    s = dot(key_part(x, key), q, NT)
                    if masked:
                        x_of = lax.rem(my_x + x, n_x) * n_y
                        s = jnp.where(key_pos + x_of <= query_pos, s, NEG_FILL)
                    s_keep[slot, x] = s
                    top = jnp.maximum(top, jnp.max(s, axis=0, keepdims=True))
                shrink = jnp.exp2((high - top) * power)
                mass = mass * shrink
                mean = mean * shrink
                for x in range(n_x):
                    dp = dot(value_part(x, key), g, NT)
                    p_keep[slot, x] = dp
                    e = jnp.exp2((s_keep[slot, x] - top) * power)
                    mass = mass + jnp.sum(e, axis=0, keepdims=True)
                    mean = mean + jnp.sum(e * dp, axis=0, keepdims=True)
                return top, mass, mean

            none = jnp.zeros((1, span), f32)
            stats = score(block, (none + NEG_FILL, none, none), True)
            stats = lax.fori_loop(low, block, lambda key, stats: score(key, stats, False), stats)
            high, mass, mean = stats
            norm = high * power + jnp.log2(mass)
            delta = mean / mass

            def back(key, fresh):
                slot = key - low
                total = None
                for x in range(n_x):
                    p = jnp.exp2(s_keep[slot, x] * power - norm)
                    ds = (p * (p_keep[slot, x] - delta)).astype(bf16)
                    dv = dot(p.astype(bf16), g, NN)
                    dk = dot(ds, q, NN)
                    dq = dot(ds, key_part(x, key), TN)
                    total = dq if total is None else total + dq
                    if fresh:
                        v_acc[x, key] = dv
                        k_acc[x, key] = dk
                    else:
                        v_acc[x, key] += dv
                        k_acc[x, key] += dk
                if fresh:
                    q_acc[...] = total
                else:
                    q_acc[...] += total

            back(block, True)
            lax.fori_loop(low, block, lambda key, _: (back(key, False), 0)[1], 0)
            for h in range(heads):
                mine = (q_acc[h * part:(h + 1) * part, :] * factor).astype(bf16)
                dq_ref[:, pl.ds(at, groups), h * head_dim:(h + 1) * head_dim] = mine.reshape(n_y, groups, head_dim)

            if has_carry:
                after = first_ref[jnp.minimum(block + 1, cap - 1)]

                @pl.when((block == cap - 1) | (after < 0) | (after > block))
                def _():
                    lax.fori_loop(low, block + 1, lambda key, _: (put(key), 0)[1], 0)
        return 0

    lax.fori_loop(begin, begin + count, one_block, 0)


def attention(first, my_x, packed, keys, begin, count, limit, carry=None):
    groups, n_y, rows, head_dim = packed.shape
    n_x = HEADS // KV_HEADS
    cap = first.shape[0]
    part = groups * n_y
    span = n_x * part
    vmem = pl.BlockSpec(memory_space=pltpu.VMEM)
    smem = pl.BlockSpec(memory_space=pltpu.SMEM)
    shape = jax.ShapeDtypeStruct
    dq = shape((n_y, count * groups, n_x * head_dim), bf16)
    slots = MAXDOC if carry is not None else min(MAXDOC, count)
    scratch = [
        pltpu.VMEM((2 * count, span, head_dim), bf16),
        pltpu.VMEM((slots, n_x, part, span), f32),
        pltpu.VMEM((slots, n_x, part, span), f32),
    ]
    sums = (n_x, begin + count, part, head_dim)
    total = [pltpu.VMEM((span, head_dim), f32)]
    if carry is None:
        out = (dq, shape(sums, f32), shape(sums, f32))
        carry = ()
        scratch = scratch + total
    else:
        one = cap * groups
        out = (dq,) + tuple(shape((n_y, rows, head_dim), bf16) for rows in (2 * one, 2 * one, 2 * one, one, one))
        scratch = scratch + [pltpu.VMEM(sums, f32)] * 2 + total
    pairs = count * 2
    return pl.pallas_call(
        functools.partial(attention_kernel, begin, count, cap, n_x, bool(carry)),
        out_shape=out,
        in_specs=[smem, smem] + [vmem] * (1 + len(keys) + len(carry)),
        out_specs=(vmem,) * len(out),
        scratch_shapes=scratch,
        compiler_params=pltpu.CompilerParams(vmem_limit_bytes=limit * 2**20),
        cost_estimate=pl.CostEstimate(
            flops=pairs * 10 * span * span * head_dim, bytes_accessed=8 * 2**20, transcendentals=pairs * 2 * span * span),
        name="attention",
    )(first, my_x, packed, *keys, *carry)


def pack_kernel(begin, count, cap, with_kv, *refs):
    lens_ref, groups_ref, offsets_ref, q_ref, g_ref = refs[:5]
    if with_kv:
        k_ref, v_ref, out_ref, pick, pick_kv = refs[5:]
    else:
        out_ref, pick = refs[5:]
    n_grp = out_ref.shape[0]
    units = q_ref.shape[0]
    head_dim = out_ref.shape[3]
    per = 2 * count

    @pl.when(pl.program_id(0) == 0)
    def _():
        lens = lens_ref[...]
        docs = lens.shape[1]
        before = lax.broadcasted_iota(jnp.int32, (docs, docs), 0) < lax.broadcasted_iota(jnp.int32, (docs, docs), 1)
        many = jnp.broadcast_to(lens, (16, docs)).astype(f32).astype(bf16)
        start = dot(many, jnp.where(before, 1.0, 0.0).astype(bf16), NN)[:1].astype(jnp.int32)
        low = groups_ref[...] * cap + offsets_ref[...]

        def choose(first, blocks, into):
            rows = n_grp * 2 * blocks
            row = lax.broadcasted_iota(jnp.int32, (rows, docs), 0)
            place = row // (2 * blocks) * cap + first + row % blocks
            inside = (place >= low) & (place < low + lens)
            source = jnp.sum(jnp.where(inside, start - low + place + 1, 0), axis=1, keepdims=True) - 1
            kind = lax.broadcasted_iota(jnp.int32, (rows, 1), 0) // blocks % 2
            wanted = jnp.where(source >= 0, source + kind * units, -1)
            column = lax.broadcasted_iota(jnp.int32, (rows, 2 * units), 1)
            into[...] = jnp.where(column == wanted, 1.0, 0.0).astype(bf16)

        choose(begin, count, pick)
        if with_kv:
            choose(0, cap, pick_kv)

    moved = dot(pick[...], jnp.concatenate([q_ref[...], g_ref[...]], axis=0), NN)
    heads = moved.shape[1] // head_dim
    for h in range(heads):
        slab = moved[:, h * head_dim:(h + 1) * head_dim].reshape(n_grp, per, head_dim)
        out_ref[:, 0, h * per:(h + 1) * per, :] = slab.astype(bf16)
    if with_kv:
        both = dot(pick_kv[...], jnp.concatenate([k_ref[...], v_ref[...]], axis=0), NN)
        out_ref[:, 0, heads * per:, :] = both.reshape(n_grp, 2 * cap, head_dim).astype(bf16)


def pack(tables, q, g, kv, n_grp, n_y, begin, count, cap):
    units = q.shape[0]
    heads = q.shape[1] // (n_y * HEAD_DIM)
    rows = heads * 2 * count + (2 * cap if kv else 0)
    table = pl.BlockSpec((1, tables[0].shape[1]), lambda y: (0, 0))
    wide = pl.BlockSpec((units, heads * HEAD_DIM), lambda y: (0, y))
    thin = pl.BlockSpec((units, HEAD_DIM), lambda y: (0, y))
    scratch = [pltpu.VMEM((n_grp * 2 * count, 2 * units), bf16)]
    if kv:
        scratch.append(pltpu.VMEM((n_grp * 2 * cap, 2 * units), bf16))
    return pl.pallas_call(
        functools.partial(pack_kernel, begin, count, cap, bool(kv)),
        out_shape=jax.ShapeDtypeStruct((n_grp, n_y, rows, HEAD_DIM), bf16),
        grid=(n_y,),
        in_specs=[table] * 3 + [wide] * 2 + [thin] * len(kv),
        out_specs=pl.BlockSpec((n_grp, 1, rows, HEAD_DIM), lambda y: (0, y, 0, 0)),
        scratch_shapes=scratch,
        compiler_params=pltpu.CompilerParams(vmem_limit_bytes=LIMIT * 2**20),
        cost_estimate=pl.CostEstimate(flops=2 * 10**9, bytes_accessed=6 * 2**20, transcendentals=0),
        name="pack",
    )(*tables, q, g, *kv)


def add_kernel(own_ref, up_ref, down_ref, k_ref, v_ref, out_ref):
    rows = k_ref.shape[1]
    low, high = slice(0, rows), slice(rows, 2 * rows)
    dk = own_ref[:, low].astype(f32) + down_ref[:, low].astype(f32) + k_ref[...].astype(f32)
    dv = own_ref[:, high].astype(f32) + up_ref[:, high].astype(f32) + v_ref[...].astype(f32)
    out_ref[:, low] = dk.astype(bf16)
    out_ref[:, high] = dv.astype(bf16)


def add_up(*parts):
    vmem = pl.BlockSpec(memory_space=pltpu.VMEM)
    return pl.pallas_call(
        add_kernel,
        out_shape=jax.ShapeDtypeStruct(parts[0].shape, bf16),
        in_specs=[vmem] * len(parts),
        out_specs=vmem,
        compiler_params=pltpu.CompilerParams(vmem_limit_bytes=16 * 2**20),
        name="add_up",
    )(*parts)


def lay_kernel(pieces, *refs):
    sources = 1 + max(piece[0] for piece in pieces)
    for source, row, rows, target, at in pieces:
        taken, out_ref = refs[source], refs[sources + target]
        n_y, _, width = taken.shape
        for y in range(n_y):
            out_ref[at:at + rows, y * width:(y + 1) * width] = taken[y, row:row + rows, :]


def lay_out(arrays, pieces, shapes):
    vmem = pl.BlockSpec(memory_space=pltpu.VMEM)
    return pl.pallas_call(
        functools.partial(lay_kernel, pieces),
        out_shape=tuple(jax.ShapeDtypeStruct(shape, bf16) for shape in shapes),
        in_specs=[vmem] * len(arrays),
        out_specs=(vmem,) * len(shapes),
        compiler_params=pltpu.CompilerParams(vmem_limit_bytes=16 * 2**20),
        name="lay_out",
    )(*arrays)


def first_blocks(doc_lengths, doc_groups, doc_offsets, cap):
    place = jnp.arange(cap, dtype=jnp.int32)[:, None]
    here = (doc_groups == lax.axis_index("grp"))[None, :]
    member = here & (doc_offsets[None, :] <= place) & (place < (doc_offsets + doc_lengths)[None, :])
    return jnp.sum(jnp.where(member, doc_offsets[None, :] + 1, 0), axis=1) - 1


def step(array, by):
    n_x = lax.axis_size("x")
    return lax.ppermute(array, "x", [(i, (i + by) % n_x) for i in range(n_x)])


def on_device(q_src, k_src, v_src, grad_src, doc_lengths, doc_groups, doc_offsets):
    n_grp, n_x, n_y = lax.axis_size("grp"), lax.axis_size("x"), lax.axis_size("y")
    units = q_src.shape[0]
    docs = doc_lengths.shape[0]
    cap = docs // n_grp
    split = EARLY
    tables = tuple(table.reshape(1, docs) for table in (doc_lengths, doc_groups, doc_offsets))
    q, k, v, g = (array.reshape(units, array.shape[-1]) for array in (q_src, k_src, v_src, grad_src))

    def exchange(message):
        rows = message.shape[2]
        home = lax.all_to_all(message.reshape(n_grp * n_y, rows, HEAD_DIM), ("grp", "y"), 0, 0, tiled=True)
        return home.reshape(n_grp, n_y, rows, HEAD_DIM)

    early = exchange(pack(tables, q, g, (k, v), n_grp, n_y, 0, split, cap))
    late = exchange(pack(tables, q, g, (), n_grp, n_y, split, cap - split, cap))

    at = n_x * 2 * split
    own = early[:, :, at:at + 2 * cap].transpose(2, 1, 0, 3).reshape(2 * cap, n_y * n_grp, HEAD_DIM)
    left, right = step(own, 1), step(own, -1)
    keys = (own, right, left, step(left[:cap], 1), step(right[cap:], -1))

    first = first_blocks(doc_lengths, doc_groups, doc_offsets, cap)
    my_x = lax.axis_index("x").astype(jnp.int32).reshape(1)
    dq_early, k_sums, v_sums = attention(first, my_x, early, keys, 0, split, 60)
    dq_late, own, up, down, dk, dv = attention(first, my_x, late, keys, split, cap - split, 60, (k_sums, v_sums))

    dq_early = lax.all_to_all(dq_early, "y", 0, 0, tiled=True)
    dq_late = lax.all_to_all(dq_late, "y", 0, 0, tiled=True)

    def joined(mine, came):
        return (mine.astype(f32) + came.astype(f32)).astype(bf16)

    rows = cap * n_grp
    up, down = step(up, 1), step(down, -1)
    k_in, v_in = step(joined(dk, up[:, :rows]), 1), step(joined(dv, down[:, rows:]), -1)
    sums = add_up(own, up, down, k_in, v_in)
    sums = lax.all_to_all(sums, "y", 0, 0, tiled=True)

    near = split * n_grp
    (dq_out,) = lay_out(
        (dq_early, dq_late), ((0, 0, near, 0, 0), (1, 0, rows - near, 0, near)), ((rows, HEADS * HEAD_DIM),))
    dk_out, dv_out = lay_out((sums,), ((0, 0, rows, 0, 0), (0, rows, rows, 1, 0)), ((rows, KV_HEADS * HEAD_DIM),) * 2)
    return tuple(array.reshape(1, rows, 1, array.shape[-1]) for array in (dq_out, dk_out, dv_out))


def solution(mesh):
    groups = mesh.shape["grp"]
    split = Mesh(mesh.devices.reshape(groups, HEADS // KV_HEADS, KV_HEADS), ("grp", "x", "y"))
    placed = P(None, "grp", ("x", "y"), None)
    out = P("grp", None, ("x", "y"), None)
    return jax.shard_map(
        on_device,
        mesh=split,
        in_specs=(placed,) * 4 + (P(),) * 3,
        out_specs=(out,) * 3,
        check_vma=False,
    )
```

```python
import functools
import math

import jax
import jax.numpy as jnp
from jax import lax
from jax.experimental import pallas as pl
from jax.experimental.pallas import tpu as pltpu
from jax.sharding import Mesh, PartitionSpec as P

HEADS = 32
KV_HEADS = 8
HEAD_DIM = 128
MAXDOC = 5
EARLY = 5
QUAD = 4
NN = (((1,), (0,)), ((), ()))
NT = (((1,), (1,)), ((), ()))
TN = (((0,), (0,)), ((), ()))
f32 = jnp.float32
bf16 = jnp.bfloat16
NEG_FILL = -1e30


def dot(a, b, dims):
    return lax.dot_general(a, b, dims, preferred_element_type=f32)


def attention_kernel(begin, count, cap, early, n_x, has_carry, *refs):
    first_ref, where_ref, in_ref = refs[:3]
    near = refs[3:8]
    if has_carry:
        late_ref, k_carry, v_carry, dq_ref = refs[8:12]
        dk_refs, dv_refs = refs[12:12 + n_x], refs[12 + n_x:12 + 2 * n_x]
        refs = refs[12 + 2 * n_x:]
        queries, keys, values, s_keep, p_keep, q_acc, sem, k_acc, v_acc = refs
    else:
        dq_ref, k_acc, v_acc, queries, keys, values, s_keep, p_keep, q_acc, sem = refs[8:]
    groups, n_y, _, head_dim = in_ref.shape
    heads = n_x
    part = groups * n_y
    span = heads * part
    rest = cap - early
    factor = 1.0 / math.sqrt(head_dim)
    power = math.log2(math.e) * factor
    my_x = where_ref[0]

    moves = []
    own, right, left, far_k, far_v = near
    for slot, k_from, k_row, v_from, v_row in (
        (0, own, 0, own, early), (1, right, 0, right, early), (2, far_k, 0, far_v, 0), (3, left, 0, left, early)):
        moves.append((k_from.at[pl.ds(k_row, early)], keys.at[slot, pl.ds(0, early)]))
        moves.append((v_from.at[pl.ds(v_row, early)], values.at[slot, pl.ds(0, early)]))
    if has_carry:
        for slot in range(n_x):
            x = lax.rem(my_x + slot, n_x)
            moves.append((late_ref.at[x, pl.ds(0, rest)], keys.at[slot, pl.ds(early, rest)]))
            moves.append((late_ref.at[x, pl.ds(rest, rest)], values.at[slot, pl.ds(early, rest)]))
        moves.append((k_carry, k_acc.at[:, pl.ds(0, early)]))
        moves.append((v_carry, v_acc.at[:, pl.ds(0, early)]))
    copies = [pltpu.make_async_copy(source, target, sem.at[i]) for i, (source, target) in enumerate(moves)]
    for copy in copies:
        copy.start()

    per = 2 * QUAD
    mixed = groups * per
    row = lax.broadcasted_iota(jnp.int32, (mixed, mixed), 0)
    col = lax.broadcasted_iota(jnp.int32, (mixed, mixed), 1)
    turn = jnp.where((row // groups == col % per) & (row % groups == col // per), 1.0, 0.0).astype(bf16)
    quads, ones = count // QUAD, count % QUAD

    def sort_y(y, _):
        def turned(starts):
            taken = jnp.concatenate(
                [in_ref[:, y, start:start + per, :].reshape(mixed, head_dim) for start in starts], axis=1)
            out = dot(turn, taken, NN).astype(bf16)
            return [out[:, i * head_dim:(i + 1) * head_dim].reshape(per, groups, head_dim) for i in range(len(starts))]

        at = [pl.ds(pl.multiple_of(h * part + y * groups, groups), groups) for h in range(heads)]
        for j in range(quads):
            slabs = turned([(j * heads + h) * per for h in range(heads)])
            for h in range(heads):
                for kind in range(2):
                    to = kind * count + j * QUAD
                    queries[to:to + QUAD, at[h], :] = slabs[h][kind * QUAD:(kind + 1) * QUAD]
        if ones:
            slabs = turned([(quads * heads + i) * per for i in range(ones)])
            for i in range(ones):
                for h in range(heads):
                    for kind in range(2):
                        queries[kind * count + quads * QUAD + i, at[h], :] = slabs[i][2 * h + kind]
        return 0

    lax.fori_loop(0, n_y, sort_y, 0)
    for copy in copies:
        copy.wait()

    def put(block):
        at = pl.multiple_of(block * groups, groups)
        for x in range(n_x):
            dk_refs[x][:, pl.ds(at, groups), :] = (k_acc[x, block] * factor).astype(bf16).reshape(n_y, groups, head_dim)
            dv_refs[x][:, pl.ds(at, groups), :] = v_acc[x, block].astype(bf16).reshape(n_y, groups, head_dim)

    if has_carry:
        low = first_ref[begin]
        low = jnp.where(low < 0, begin, jnp.minimum(low, begin))
        lax.fori_loop(0, low, lambda block, _: (put(block), 0)[1], 0)

    key_row = lax.broadcasted_iota(jnp.int32, (part, span), 0)
    query_col = lax.broadcasted_iota(jnp.int32, (part, span), 1) % part
    key_pos = (key_row % groups) * (n_x * n_y) + key_row // groups
    query_pos = (query_col % groups) * (n_x * n_y) + query_col // groups + my_x * n_y

    def one_block(block, _):
        low = first_ref[block]
        local = block - begin
        at = pl.multiple_of(local * groups, groups)

        @pl.when(low < 0)
        def _():
            dq_ref[:, pl.ds(at, groups), :] = jnp.zeros((n_y, groups, heads * head_dim), bf16)
            zero = jnp.zeros((part, head_dim), f32)
            for x in range(n_x):
                k_acc[x, block] = zero
                v_acc[x, block] = zero
            if has_carry:
                put(block)

        @pl.when(low >= 0)
        def _():
            q = queries[local]
            g = queries[count + local]

            def score(key, stats, masked):
                high, mass, mean = stats
                slot = key - low
                top = high
                for x in range(n_x):
                    s = dot(keys[x, key], q, NT)
                    if masked:
                        x_of = lax.rem(my_x + x, n_x) * n_y
                        s = jnp.where(key_pos + x_of <= query_pos, s, NEG_FILL)
                    s_keep[slot, x] = s
                    top = jnp.maximum(top, jnp.max(s, axis=0, keepdims=True))
                shrink = jnp.exp2((high - top) * power)
                mass = mass * shrink
                mean = mean * shrink
                for x in range(n_x):
                    dp = dot(values[x, key], g, NT)
                    p_keep[slot, x] = dp
                    e = jnp.exp2((s_keep[slot, x] - top) * power)
                    mass = mass + jnp.sum(e, axis=0, keepdims=True)
                    mean = mean + jnp.sum(e * dp, axis=0, keepdims=True)
                return top, mass, mean

            none = jnp.zeros((1, span), f32)
            stats = score(block, (none + NEG_FILL, none, none), True)
            stats = lax.fori_loop(low, block, lambda key, stats: score(key, stats, False), stats)
            high, mass, mean = stats
            norm = high * power + jnp.log2(mass)
            delta = mean / mass

            def back(key, fresh):
                slot = key - low
                total = None
                for x in range(n_x):
                    p = jnp.exp2(s_keep[slot, x] * power - norm)
                    ds = (p * (p_keep[slot, x] - delta)).astype(bf16)
                    dv = dot(p.astype(bf16), g, NN)
                    dk = dot(ds, q, NN)
                    dq = dot(ds, keys[x, key], TN)
                    total = dq if total is None else total + dq
                    if fresh:
                        v_acc[x, key] = dv
                        k_acc[x, key] = dk
                    else:
                        v_acc[x, key] += dv
                        k_acc[x, key] += dk
                if fresh:
                    q_acc[...] = total
                else:
                    q_acc[...] += total

            back(block, True)
            lax.fori_loop(low, block, lambda key, _: (back(key, False), 0)[1], 0)
            for h in range(heads):
                mine = (q_acc[h * part:(h + 1) * part, :] * factor).astype(bf16)
                dq_ref[:, pl.ds(at, groups), h * head_dim:(h + 1) * head_dim] = mine.reshape(n_y, groups, head_dim)

            if has_carry:
                after = first_ref[jnp.minimum(block + 1, cap - 1)]

                @pl.when((block == cap - 1) | (after < 0) | (after > block))
                def _():
                    lax.fori_loop(low, block + 1, lambda key, _: (put(key), 0)[1], 0)
        return 0

    lax.fori_loop(begin, begin + count, one_block, 0)


def attention(first, my_x, packed, near, begin, count, late=None, carry=()):
    groups, n_y, _, head_dim = packed.shape
    n_x = HEADS // KV_HEADS
    cap = first.shape[0]
    early = near[3].shape[0]
    part = groups * n_y
    span = n_x * part
    vmem = pl.BlockSpec(memory_space=pltpu.VMEM)
    smem = pl.BlockSpec(memory_space=pltpu.SMEM)
    anywhere = pl.BlockSpec(memory_space=pl.ANY)
    shape = jax.ShapeDtypeStruct
    dq = shape((n_y, count * groups, n_x * head_dim), bf16)
    has_carry = late is not None
    reach = begin + count
    slots = min(MAXDOC, reach)
    sums = (n_x, reach, part, head_dim)
    more = (late, *carry) if has_carry else ()
    scratch = [
        pltpu.VMEM((2 * count, span, head_dim), bf16),
        pltpu.VMEM((n_x, reach, part, head_dim), bf16),
        pltpu.VMEM((n_x, reach, part, head_dim), bf16),
        pltpu.VMEM((slots, n_x, part, span), f32),
        pltpu.VMEM((slots, n_x, part, span), f32),
        pltpu.VMEM((span, head_dim), f32),
        pltpu.SemaphoreType.DMA((2 * n_x + (2 * n_x + 2 if has_carry else 0),)),
    ]
    if has_carry:
        out = (dq,) + (shape((n_y, cap * groups, head_dim), bf16),) * (2 * n_x)
        scratch = scratch + [pltpu.VMEM(sums, f32)] * 2
    else:
        out = (dq, shape(sums, f32), shape(sums, f32))
    pairs = count * 2
    return pl.pallas_call(
        functools.partial(attention_kernel, begin, count, cap, early, n_x, has_carry),
        out_shape=out,
        in_specs=[smem, smem, vmem] + [anywhere] * (len(near) + len(more)),
        out_specs=(vmem,) * len(out),
        scratch_shapes=scratch,
        compiler_params=pltpu.CompilerParams(vmem_limit_bytes=60 * 2**20),
        cost_estimate=pl.CostEstimate(
            flops=pairs * 10 * span * span * head_dim, bytes_accessed=8 * 2**20, transcendentals=pairs * 2 * span * span),
        name="attention",
    )(first, my_x, packed, *near, *more)


def pack_kernel(begin, count, cap, early, *refs):
    lens_ref, groups_ref, offsets_ref, q_ref, g_ref = refs[:5]
    if early:
        k_ref, v_ref, out_ref, pick_quad, pick_one, pick_kv = refs[5:]
    else:
        out_ref, pick_quad, pick_one = refs[5:]
    n_grp, _, _, head_dim = out_ref.shape
    units = q_ref.shape[0]
    heads = q_ref.shape[1] // head_dim
    per = 2 * QUAD
    quads, ones = count // QUAD, count % QUAD

    @pl.when(pl.program_id(0) == 0)
    def _():
        lens = lens_ref[...]
        docs = lens.shape[1]
        before = lax.broadcasted_iota(jnp.int32, (docs, docs), 0) < lax.broadcasted_iota(jnp.int32, (docs, docs), 1)
        many = jnp.broadcast_to(lens, (16, docs)).astype(f32).astype(bf16)
        start = dot(many, jnp.where(before, 1.0, 0.0).astype(bf16), NN)[:1].astype(jnp.int32)
        low = groups_ref[...] * cap + offsets_ref[...]

        def choose(rows, block, shift, width):
            place = lax.broadcasted_iota(jnp.int32, (n_grp * rows, docs), 0)
            place = place // rows * cap + block(place % rows)
            inside = (place >= low) & (place < low + lens)
            source = jnp.sum(jnp.where(inside, start - low + place + 1, 0), axis=1, keepdims=True) - 1
            row = lax.broadcasted_iota(jnp.int32, (n_grp * rows, 1), 0) % rows
            wanted = jnp.where(source >= 0, source + shift(row) * units, -1)
            column = lax.broadcasted_iota(jnp.int32, (n_grp * rows, width * units), 1)
            return jnp.where(column == wanted, 1.0, 0.0).astype(bf16)

        for j in range(quads):
            pick_quad[j] = choose(per, lambda r: begin + j * QUAD + r % QUAD, lambda r: r // QUAD, 2)
        for i in range(ones):
            pick_one[i] = choose(per, lambda r: r * 0 + (begin + quads * QUAD + i), lambda r: r, 2 * heads)
        if early:
            rest = cap - early
            pick_kv[...] = choose(
                2 * cap,
                lambda r: jnp.where(r < 2 * early, r % early, early + (r - 2 * early) % rest),
                lambda r: jnp.where(r < 2 * early, r // early, (r - 2 * early) // rest),
                2)

    both = jnp.concatenate([q_ref[...], g_ref[...]], axis=0)
    for j in range(quads):
        moved = dot(pick_quad[j], both, NN)
        for h in range(heads):
            at = (j * heads + h) * per
            slab = moved[:, h * head_dim:(h + 1) * head_dim].reshape(n_grp, per, head_dim)
            out_ref[:, 0, at:at + per, :] = slab.astype(bf16)
    if ones:
        tall = jnp.concatenate([both[:, h * head_dim:(h + 1) * head_dim] for h in range(heads)], axis=0)
    for i in range(ones):
        at = (quads * heads + i) * per
        out_ref[:, 0, at:at + per, :] = dot(pick_one[i], tall, NN).reshape(n_grp, per, head_dim).astype(bf16)
    if early:
        both = dot(pick_kv[...], jnp.concatenate([k_ref[...], v_ref[...]], axis=0), NN)
        out_ref[:, 0, 2 * heads * count:, :] = both.reshape(n_grp, 2 * cap, head_dim).astype(bf16)


def pack(tables, q, g, kv, n_grp, n_y, begin, count, cap):
    units = q.shape[0]
    heads = q.shape[1] // (n_y * HEAD_DIM)
    rows = heads * 2 * count + (2 * cap if kv else 0)
    table = pl.BlockSpec((1, tables[0].shape[1]), lambda y: (0, 0))
    wide = pl.BlockSpec((units, heads * HEAD_DIM), lambda y: (0, y))
    thin = pl.BlockSpec((units, HEAD_DIM), lambda y: (0, y))
    tall = n_grp * 2 * QUAD
    scratch = [
        pltpu.VMEM((count // QUAD, tall, 2 * units), bf16),
        pltpu.VMEM((max(1, count % QUAD), tall, 2 * heads * units), bf16),
    ]
    if kv:
        scratch.append(pltpu.VMEM((n_grp * 2 * cap, 2 * units), bf16))
    return pl.pallas_call(
        functools.partial(pack_kernel, begin, count, cap, count if kv else 0),
        out_shape=jax.ShapeDtypeStruct((n_grp, n_y, rows, HEAD_DIM), bf16),
        grid=(n_y,),
        in_specs=[table] * 3 + [wide] * 2 + [thin] * len(kv),
        out_specs=pl.BlockSpec((n_grp, 1, rows, HEAD_DIM), lambda y: (0, y, 0, 0)),
        scratch_shapes=scratch,
        compiler_params=pltpu.CompilerParams(vmem_limit_bytes=60 * 2**20),
        cost_estimate=pl.CostEstimate(flops=2 * 10**9, bytes_accessed=6 * 2**20, transcendentals=0),
        name="pack",
    )(*tables, q, g, *kv)


def add_kernel(*refs):
    out_ref = refs[-1]
    rows = out_ref.shape[1] // 2
    for half in range(2):
        a, b, c = refs[3 * half:3 * half + 3]
        total = a[...].astype(f32) + b[...].astype(f32) + c[...].astype(f32)
        out_ref[:, half * rows:(half + 1) * rows, :] = total.astype(bf16)


def add_up(dk_parts, dv_parts):
    n_y, rows, head_dim = dk_parts[0].shape
    vmem = pl.BlockSpec(memory_space=pltpu.VMEM)
    return pl.pallas_call(
        add_kernel,
        out_shape=jax.ShapeDtypeStruct((n_y, 2 * rows, head_dim), bf16),
        in_specs=[vmem] * 6,
        out_specs=vmem,
        compiler_params=pltpu.CompilerParams(vmem_limit_bytes=16 * 2**20),
        name="add_up",
    )(*dk_parts, *dv_parts)


def lay_kernel(pieces, *refs):
    sources = 1 + max(piece[0] for piece in pieces)
    for source, row, rows, target, at in pieces:
        taken, out_ref = refs[source], refs[sources + target]
        n_y, _, width = taken.shape
        for y in range(n_y):
            out_ref[at:at + rows, y * width:(y + 1) * width] = taken[y, row:row + rows, :]


def lay_out(arrays, pieces, shapes):
    vmem = pl.BlockSpec(memory_space=pltpu.VMEM)
    return pl.pallas_call(
        functools.partial(lay_kernel, pieces),
        out_shape=tuple(jax.ShapeDtypeStruct(shape, bf16) for shape in shapes),
        in_specs=[vmem] * len(arrays),
        out_specs=(vmem,) * len(shapes),
        compiler_params=pltpu.CompilerParams(vmem_limit_bytes=16 * 2**20),
        name="lay_out",
    )(*arrays)


def first_blocks(doc_lengths, doc_groups, doc_offsets, cap):
    place = jnp.arange(cap, dtype=jnp.int32)[:, None]
    here = (doc_groups == lax.axis_index("grp"))[None, :]
    member = here & (doc_offsets[None, :] <= place) & (place < (doc_offsets + doc_lengths)[None, :])
    return jnp.sum(jnp.where(member, doc_offsets[None, :] + 1, 0), axis=1) - 1


def step(array, by):
    n_x = lax.axis_size("x")
    return lax.ppermute(array, "x", [(i, (i + by) % n_x) for i in range(n_x)])


def on_device(q_src, k_src, v_src, grad_src, doc_lengths, doc_groups, doc_offsets):
    n_grp, n_x, n_y = lax.axis_size("grp"), lax.axis_size("x"), lax.axis_size("y")
    units = q_src.shape[0]
    docs = doc_lengths.shape[0]
    cap = docs // n_grp
    split = EARLY
    tables = tuple(table.reshape(1, docs) for table in (doc_lengths, doc_groups, doc_offsets))
    q, k, v, g = (array.reshape(units, array.shape[-1]) for array in (q_src, k_src, v_src, grad_src))

    def exchange(message):
        rows = message.shape[2]
        home = lax.all_to_all(message.reshape(n_grp * n_y, rows, HEAD_DIM), ("grp", "y"), 0, 0, tiled=True)
        return home.reshape(n_grp, n_y, rows, HEAD_DIM)

    early = exchange(pack(tables, q, g, (k, v), n_grp, n_y, 0, split, cap))
    late = exchange(pack(tables, q, g, (), n_grp, n_y, split, cap - split, cap))

    at = 2 * n_x * split

    def keys_of(first_row, rows):
        taken = early[:, :, at + first_row:at + first_row + rows]
        return taken.transpose(2, 1, 0, 3).reshape(rows, n_y * n_grp, HEAD_DIM)

    own = keys_of(0, 2 * split)
    left, right = step(own, 1), step(own, -1)
    near = (own, right, left, step(left[:split], 1), step(right[split:], -1))
    far = lax.all_gather(keys_of(2 * split, 2 * (cap - split)), "x", axis=0)

    first = first_blocks(doc_lengths, doc_groups, doc_offsets, cap)
    my_x = lax.axis_index("x").astype(jnp.int32).reshape(1)
    dq_early, k_sums, v_sums = attention(first, my_x, early, near, 0, split)
    dq_late, *grads = attention(first, my_x, late, near, split, cap - split, far, (k_sums, v_sums))
    dk, dv = grads[:n_x], grads[n_x:]

    dq_early = lax.all_to_all(dq_early, "y", 0, 0, tiled=True)
    dq_late = lax.all_to_all(dq_late, "y", 0, 0, tiled=True)

    def joined(mine, came):
        return (mine.astype(f32) + came.astype(f32)).astype(bf16)

    k_far, v_far = step(dk[2], 1), step(dv[2], -1)
    v_up, k_down = step(dv[1], 1), step(dk[3], -1)
    k_up, v_down = step(joined(dk[1], k_far), 1), step(joined(dv[3], v_far), -1)
    sums = add_up((dk[0], k_up, k_down), (dv[0], v_up, v_down))
    sums = lax.all_to_all(sums, "y", 0, 0, tiled=True)

    rows, near = cap * n_grp, split * n_grp
    (dq_out,) = lay_out(
        (dq_early, dq_late), ((0, 0, near, 0, 0), (1, 0, rows - near, 0, near)), ((rows, HEADS * HEAD_DIM),))
    dk_out, dv_out = lay_out((sums,), ((0, 0, rows, 0, 0), (0, rows, rows, 1, 0)), ((rows, KV_HEADS * HEAD_DIM),) * 2)
    return tuple(array.reshape(1, rows, 1, array.shape[-1]) for array in (dq_out, dk_out, dv_out))


def solution(mesh):
    groups = mesh.shape["grp"]
    split = Mesh(mesh.devices.reshape(groups, HEADS // KV_HEADS, KV_HEADS), ("grp", "x", "y"))
    placed = P(None, "grp", ("x", "y"), None)
    out = P("grp", None, ("x", "y"), None)
    return jax.shard_map(
        on_device,
        mesh=split,
        in_specs=(placed,) * 4 + (P(),) * 3,
        out_specs=(out,) * 3,
        check_vma=False,
    )
```

```python
import functools
import math

import jax
import jax.numpy as jnp
from jax import lax
from jax.experimental import pallas as pl
from jax.experimental.pallas import tpu as pltpu
from jax.sharding import Mesh, PartitionSpec as P

HEADS = 32
KV_HEADS = 8
HEAD_DIM = 128
MAXDOC = 5
EARLY = 5
QUAD = 4
AT_ONCE = 4
NN = (((1,), (0,)), ((), ()))
NT = (((1,), (1,)), ((), ()))
TN = (((0,), (0,)), ((), ()))
f32 = jnp.float32
bf16 = jnp.bfloat16
NEG_FILL = -1e30


def dot(a, b, dims):
    return lax.dot_general(a, b, dims, preferred_element_type=f32)


def attention_kernel(begin, count, cap, early, n_x, has_carry, *refs):
    first_ref, where_ref, in_ref = refs[:3]
    near = refs[3:3 + n_x]
    if has_carry:
        far = refs[3 + n_x:3 + 2 * n_x]
        k_carry, v_carry, dq_ref = refs[3 + 2 * n_x:6 + 2 * n_x]
        refs = refs[6 + 2 * n_x:]
        dk_refs, dv_refs = refs[:n_x], refs[n_x:2 * n_x]
        refs = refs[2 * n_x:]
        queries, keys, values, s_keep, p_keep, q_acc, sem, k_acc, v_acc = refs
    else:
        dq_ref, k_acc, v_acc, queries, keys, values, s_keep, p_keep, q_acc, sem = refs[3 + n_x:]
    groups, n_y, _, head_dim = in_ref.shape
    heads = n_x
    part = groups * n_y
    span = heads * part
    rest = cap - early
    factor = 1.0 / math.sqrt(head_dim)
    power = math.log2(math.e) * factor
    my_x = where_ref[0]

    moves = []
    for slot in range(n_x):
        moves.append((near[slot].at[pl.ds(0, early)], keys.at[slot, pl.ds(0, early)]))
        moves.append((near[slot].at[pl.ds(early, early)], values.at[slot, pl.ds(0, early)]))
    if has_carry:
        for slot in range(n_x):
            moves.append((far[slot].at[pl.ds(0, rest)], keys.at[slot, pl.ds(early, rest)]))
            moves.append((far[slot].at[pl.ds(rest, rest)], values.at[slot, pl.ds(early, rest)]))
        moves.append((k_carry, k_acc.at[:, pl.ds(0, early)]))
        moves.append((v_carry, v_acc.at[:, pl.ds(0, early)]))
    copies = [pltpu.make_async_copy(source, target, sem.at[i]) for i, (source, target) in enumerate(moves)]
    for copy in copies:
        copy.start()

    per = 2 * QUAD
    mixed = groups * per
    row = lax.broadcasted_iota(jnp.int32, (mixed, mixed), 0)
    col = lax.broadcasted_iota(jnp.int32, (mixed, mixed), 1)
    turn = jnp.where((row // groups == col % per) & (row % groups == col // per), 1.0, 0.0).astype(bf16)
    quads, ones = count // QUAD, count % QUAD

    def sort_y(y, _):
        def turned(starts):
            taken = jnp.concatenate(
                [in_ref[:, y, start:start + per, :].reshape(mixed, head_dim) for start in starts], axis=1)
            out = dot(turn, taken, NN).astype(bf16)
            return [out[:, i * head_dim:(i + 1) * head_dim].reshape(per, groups, head_dim) for i in range(len(starts))]

        at = [pl.ds(pl.multiple_of(h * part + y * groups, groups), groups) for h in range(heads)]
        for j in range(quads):
            slabs = turned([(j * heads + h) * per for h in range(heads)])
            for h in range(heads):
                for kind in range(2):
                    to = kind * count + j * QUAD
                    queries[to:to + QUAD, at[h], :] = slabs[h][kind * QUAD:(kind + 1) * QUAD]
        if ones:
            slabs = turned([(quads * heads + i) * per for i in range(ones)])
            for i in range(ones):
                for h in range(heads):
                    for kind in range(2):
                        queries[kind * count + quads * QUAD + i, at[h], :] = slabs[i][2 * h + kind]
        return 0

    lax.fori_loop(0, n_y, sort_y, 0)
    for copy in copies:
        copy.wait()

    def put(block):
        at = pl.multiple_of(block * groups, groups)
        for x in range(n_x):
            dk_refs[x][:, pl.ds(at, groups), :] = (k_acc[x, block] * factor).astype(bf16).reshape(n_y, groups, head_dim)
            dv_refs[x][:, pl.ds(at, groups), :] = v_acc[x, block].astype(bf16).reshape(n_y, groups, head_dim)

    if has_carry:
        low = first_ref[begin]
        low = jnp.where(low < 0, begin, jnp.minimum(low, begin))
        lax.fori_loop(0, low, lambda block, _: (put(block), 0)[1], 0)

    key_row = lax.broadcasted_iota(jnp.int32, (part, span), 0)
    query_col = lax.broadcasted_iota(jnp.int32, (part, span), 1) % part
    key_pos = (key_row % groups) * (n_x * n_y) + key_row // groups
    query_pos = (query_col % groups) * (n_x * n_y) + query_col // groups + my_x * n_y

    def one_block(block, _):
        low = first_ref[block]
        local = block - begin
        at = pl.multiple_of(local * groups, groups)

        @pl.when(low < 0)
        def _():
            dq_ref[:, pl.ds(at, groups), :] = jnp.zeros((n_y, groups, heads * head_dim), bf16)
            zero = jnp.zeros((part, head_dim), f32)
            for x in range(n_x):
                k_acc[x, block] = zero
                v_acc[x, block] = zero
            if has_carry:
                put(block)

        @pl.when(low >= 0)
        def _():
            q = queries[local]
            g = queries[count + local]

            def score(key, stats, masked):
                high, mass, mean = stats
                slot = key - low
                top = high
                for x in range(n_x):
                    s = dot(keys[x, key], q, NT)
                    if masked:
                        x_of = lax.rem(my_x + x, n_x) * n_y
                        s = jnp.where(key_pos + x_of <= query_pos, s, NEG_FILL)
                    s_keep[slot, x] = s
                    top = jnp.maximum(top, jnp.max(s, axis=0, keepdims=True))
                shrink = jnp.exp2((high - top) * power)
                mass = mass * shrink
                mean = mean * shrink
                for x in range(n_x):
                    dp = dot(values[x, key], g, NT)
                    p_keep[slot, x] = dp
                    e = jnp.exp2((s_keep[slot, x] - top) * power)
                    mass = mass + jnp.sum(e, axis=0, keepdims=True)
                    mean = mean + jnp.sum(e * dp, axis=0, keepdims=True)
                return top, mass, mean

            none = jnp.zeros((1, span), f32)
            stats = score(block, (none + NEG_FILL, none, none), True)
            stats = lax.fori_loop(low, block, lambda key, stats: score(key, stats, False), stats)
            high, mass, mean = stats
            norm = high * power + jnp.log2(mass)
            delta = mean / mass

            def back(key, fresh):
                slot = key - low
                total = None
                for x in range(n_x):
                    p = jnp.exp2(s_keep[slot, x] * power - norm)
                    ds = (p * (p_keep[slot, x] - delta)).astype(bf16)
                    dv = dot(p.astype(bf16), g, NN)
                    dk = dot(ds, q, NN)
                    dq = dot(ds, keys[x, key], TN)
                    total = dq if total is None else total + dq
                    if fresh:
                        v_acc[x, key] = dv
                        k_acc[x, key] = dk
                    else:
                        v_acc[x, key] += dv
                        k_acc[x, key] += dk
                if fresh:
                    q_acc[...] = total
                else:
                    q_acc[...] += total

            back(block, True)
            lax.fori_loop(low, block, lambda key, _: (back(key, False), 0)[1], 0)
            for h in range(heads):
                mine = (q_acc[h * part:(h + 1) * part, :] * factor).astype(bf16)
                dq_ref[:, pl.ds(at, groups), h * head_dim:(h + 1) * head_dim] = mine.reshape(n_y, groups, head_dim)

            if has_carry:
                after = first_ref[jnp.minimum(block + 1, cap - 1)]

                @pl.when((block == cap - 1) | (after < 0) | (after > block))
                def _():
                    lax.fori_loop(low, block + 1, lambda key, _: (put(key), 0)[1], 0)
        return 0

    lax.fori_loop(begin, begin + count, one_block, 0)


def attention(first, my_x, packed, near, begin, count, late=None, carry=()):
    groups, n_y, _, head_dim = packed.shape
    n_x = HEADS // KV_HEADS
    cap = first.shape[0]
    early = near[0].shape[0] // 2
    part = groups * n_y
    span = n_x * part
    vmem = pl.BlockSpec(memory_space=pltpu.VMEM)
    smem = pl.BlockSpec(memory_space=pltpu.SMEM)
    anywhere = pl.BlockSpec(memory_space=pl.ANY)
    shape = jax.ShapeDtypeStruct
    dq = shape((n_y, count * groups, n_x * head_dim), bf16)
    has_carry = late is not None
    reach = begin + count
    slots = min(MAXDOC, reach)
    sums = (n_x, reach, part, head_dim)
    more = (*late, *carry) if has_carry else ()
    scratch = [
        pltpu.VMEM((2 * count, span, head_dim), bf16),
        pltpu.VMEM((n_x, reach, part, head_dim), bf16),
        pltpu.VMEM((n_x, reach, part, head_dim), bf16),
        pltpu.VMEM((slots, n_x, part, span), f32),
        pltpu.VMEM((slots, n_x, part, span), f32),
        pltpu.VMEM((span, head_dim), f32),
        pltpu.SemaphoreType.DMA((2 * n_x + (2 * n_x + 2 if has_carry else 0),)),
    ]
    if has_carry:
        out = (dq,) + (shape((n_y, cap * groups, head_dim), bf16),) * (2 * n_x)
        scratch = scratch + [pltpu.VMEM(sums, f32)] * 2
    else:
        out = (dq, shape(sums, f32), shape(sums, f32))
    pairs = count * 2
    return pl.pallas_call(
        functools.partial(attention_kernel, begin, count, cap, early, n_x, has_carry),
        out_shape=out,
        in_specs=[smem, smem, vmem] + [anywhere] * (len(near) + len(more)),
        out_specs=(vmem,) * len(out),
        scratch_shapes=scratch,
        compiler_params=pltpu.CompilerParams(vmem_limit_bytes=60 * 2**20),
        cost_estimate=pl.CostEstimate(
            flops=pairs * 10 * span * span * head_dim, bytes_accessed=8 * 2**20, transcendentals=pairs * 2 * span * span),
        name="attention",
    )(first, my_x, packed, *near, *more)


def pack_kernel(begin, count, cap, early, heads, *refs):
    lens_ref, groups_ref, offsets_ref, q_ref, g_ref = refs[:5]
    if early:
        k_ref, v_ref, out_ref, pick_quad, pick_one, pick_kv = refs[5:]
    else:
        out_ref, pick_quad, pick_one = refs[5:]
    n_grp, _, _, head_dim = out_ref.shape
    units = q_ref.shape[0]
    per = 2 * QUAD
    quads, ones = count // QUAD, count % QUAD

    @pl.when(pl.program_id(0) == 0)
    def _():
        lens = lens_ref[...]
        docs = lens.shape[1]
        before = lax.broadcasted_iota(jnp.int32, (docs, docs), 0) < lax.broadcasted_iota(jnp.int32, (docs, docs), 1)
        many = jnp.broadcast_to(lens, (16, docs)).astype(f32).astype(bf16)
        start = dot(many, jnp.where(before, 1.0, 0.0).astype(bf16), NN)[:1].astype(jnp.int32)
        low = groups_ref[...] * cap + offsets_ref[...]

        def choose(rows, block, shift, width):
            place = lax.broadcasted_iota(jnp.int32, (n_grp * rows, docs), 0)
            place = place // rows * cap + block(place % rows)
            inside = (place >= low) & (place < low + lens)
            source = jnp.sum(jnp.where(inside, start - low + place + 1, 0), axis=1, keepdims=True) - 1
            row = lax.broadcasted_iota(jnp.int32, (n_grp * rows, 1), 0) % rows
            wanted = jnp.where(source >= 0, source + shift(row) * units, -1)
            column = lax.broadcasted_iota(jnp.int32, (n_grp * rows, width * units), 1)
            return jnp.where(column == wanted, 1.0, 0.0).astype(bf16)

        for j in range(quads):
            pick_quad[j] = choose(per, lambda r: begin + j * QUAD + r % QUAD, lambda r: r // QUAD, 2)
        for i in range(ones):
            pick_one[i] = choose(per, lambda r: r * 0 + (begin + quads * QUAD + i), lambda r: r, 2 * heads)
        if early:
            rest = cap - early
            pick_kv[...] = choose(
                2 * cap,
                lambda r: jnp.where(r < 2 * early, r % early, early + (r - 2 * early) % rest),
                lambda r: jnp.where(r < 2 * early, r // early, (r - 2 * early) // rest),
                2)

    width = heads * head_dim
    for y in range(q_ref.shape[1] // width):
        mine = slice(y * width, (y + 1) * width)
        both = jnp.concatenate([q_ref[:, mine], g_ref[:, mine]], axis=0)
        for j in range(quads):
            moved = dot(pick_quad[j], both, NN)
            for h in range(heads):
                at = (j * heads + h) * per
                slab = moved[:, h * head_dim:(h + 1) * head_dim].reshape(n_grp, per, head_dim)
                out_ref[:, y, at:at + per, :] = slab.astype(bf16)
        if ones:
            tall = jnp.concatenate([both[:, h * head_dim:(h + 1) * head_dim] for h in range(heads)], axis=0)
        for i in range(ones):
            at = (quads * heads + i) * per
            out_ref[:, y, at:at + per, :] = dot(pick_one[i], tall, NN).reshape(n_grp, per, head_dim).astype(bf16)
        if early:
            mine = slice(y * head_dim, (y + 1) * head_dim)
            both = dot(pick_kv[...], jnp.concatenate([k_ref[:, mine], v_ref[:, mine]], axis=0), NN)
            out_ref[:, y, 2 * heads * count:, :] = both.reshape(n_grp, 2 * cap, head_dim).astype(bf16)


def pack(tables, q, g, kv, n_grp, n_y, begin, count, cap, each=AT_ONCE):
    units = q.shape[0]
    heads = q.shape[1] // (n_y * HEAD_DIM)
    rows = heads * 2 * count + (2 * cap if kv else 0)
    table = pl.BlockSpec((1, tables[0].shape[1]), lambda y: (0, 0))
    wide = pl.BlockSpec((units, each * heads * HEAD_DIM), lambda y: (0, y))
    thin = pl.BlockSpec((units, each * HEAD_DIM), lambda y: (0, y))
    tall = n_grp * 2 * QUAD
    scratch = [
        pltpu.VMEM((count // QUAD, tall, 2 * units), bf16),
        pltpu.VMEM((max(1, count % QUAD), tall, 2 * heads * units), bf16),
    ]
    if kv:
        scratch.append(pltpu.VMEM((n_grp * 2 * cap, 2 * units), bf16))
    return pl.pallas_call(
        functools.partial(pack_kernel, begin, count, cap, count if kv else 0, heads),
        out_shape=jax.ShapeDtypeStruct((n_grp, n_y, rows, HEAD_DIM), bf16),
        grid=(n_y // each,),
        in_specs=[table] * 3 + [wide] * 2 + [thin] * len(kv),
        out_specs=pl.BlockSpec((n_grp, each, rows, HEAD_DIM), lambda y: (0, y, 0, 0)),
        scratch_shapes=scratch,
        compiler_params=pltpu.CompilerParams(vmem_limit_bytes=60 * 2**20),
        cost_estimate=pl.CostEstimate(flops=2 * 10**9, bytes_accessed=6 * 2**20, transcendentals=0),
        name="pack",
    )(*tables, q, g, *kv)


def add_kernel(*refs):
    out_ref = refs[-1]
    rows = out_ref.shape[1] // 2
    for half in range(2):
        a, b, c = refs[3 * half:3 * half + 3]
        total = a[...].astype(f32) + b[...].astype(f32) + c[...].astype(f32)
        out_ref[:, half * rows:(half + 1) * rows, :] = total.astype(bf16)


def add_up(dk_parts, dv_parts):
    n_y, rows, head_dim = dk_parts[0].shape
    vmem = pl.BlockSpec(memory_space=pltpu.VMEM)
    return pl.pallas_call(
        add_kernel,
        out_shape=jax.ShapeDtypeStruct((n_y, 2 * rows, head_dim), bf16),
        in_specs=[vmem] * 6,
        out_specs=vmem,
        compiler_params=pltpu.CompilerParams(vmem_limit_bytes=16 * 2**20),
        name="add_up",
    )(*dk_parts, *dv_parts)


def lay_kernel(pieces, *refs):
    sources = 1 + max(piece[0] for piece in pieces)
    for source, row, rows, target, at in pieces:
        taken, out_ref = refs[source], refs[sources + target]
        n_y, _, width = taken.shape
        for y in range(n_y):
            out_ref[at:at + rows, y * width:(y + 1) * width] = taken[y, row:row + rows, :]


def lay_out(arrays, pieces, shapes):
    vmem = pl.BlockSpec(memory_space=pltpu.VMEM)
    return pl.pallas_call(
        functools.partial(lay_kernel, pieces),
        out_shape=tuple(jax.ShapeDtypeStruct(shape, bf16) for shape in shapes),
        in_specs=[vmem] * len(arrays),
        out_specs=(vmem,) * len(shapes),
        compiler_params=pltpu.CompilerParams(vmem_limit_bytes=16 * 2**20),
        name="lay_out",
    )(*arrays)


def first_blocks(doc_lengths, doc_groups, doc_offsets, cap):
    place = jnp.arange(cap, dtype=jnp.int32)[:, None]
    here = (doc_groups == lax.axis_index("grp"))[None, :]
    member = here & (doc_offsets[None, :] <= place) & (place < (doc_offsets + doc_lengths)[None, :])
    return jnp.sum(jnp.where(member, doc_offsets[None, :] + 1, 0), axis=1) - 1


def step(array, by):
    n_x = lax.axis_size("x")
    return lax.ppermute(array, "x", [(i, (i + by) % n_x) for i in range(n_x)])


def on_device(q_src, k_src, v_src, grad_src, doc_lengths, doc_groups, doc_offsets):
    n_grp, n_x, n_y = lax.axis_size("grp"), lax.axis_size("x"), lax.axis_size("y")
    units = q_src.shape[0]
    docs = doc_lengths.shape[0]
    cap = docs // n_grp
    split = EARLY
    tables = tuple(table.reshape(1, docs) for table in (doc_lengths, doc_groups, doc_offsets))
    q, k, v, g = (array.reshape(units, array.shape[-1]) for array in (q_src, k_src, v_src, grad_src))

    def exchange(message):
        rows = message.shape[2]
        home = lax.all_to_all(message.reshape(n_grp * n_y, rows, HEAD_DIM), ("grp", "y"), 0, 0, tiled=True)
        return home.reshape(n_grp, n_y, rows, HEAD_DIM)

    early = exchange(pack(tables, q, g, (k, v), n_grp, n_y, 0, split, cap))
    late = exchange(pack(tables, q, g, (), n_grp, n_y, split, cap - split, cap))

    at = 2 * n_x * split

    def keys_of(first_row, rows):
        taken = early[:, :, at + first_row:at + first_row + rows]
        return taken.transpose(2, 1, 0, 3).reshape(rows, n_y * n_grp, HEAD_DIM)

    def gather(own):
        return (own, step(own, -1), step(own, 2), step(own, 1))

    near = gather(keys_of(0, 2 * split))
    other, _, _ = lax.optimization_barrier((keys_of(2 * split, 2 * (cap - split)), near[1], near[3]))
    far = gather(other)

    first = first_blocks(doc_lengths, doc_groups, doc_offsets, cap)
    my_x = lax.axis_index("x").astype(jnp.int32).reshape(1)
    dq_early, k_sums, v_sums = attention(first, my_x, early, near, 0, split)
    dq_early, *far = lax.optimization_barrier((dq_early, *far))
    dq_late, *grads = attention(first, my_x, late, near, split, cap - split, far, (k_sums, v_sums))
    dk, dv = grads[:n_x], grads[n_x:]

    dq_early = lax.all_to_all(dq_early, "y", 0, 0, tiled=True)
    dq_late = lax.all_to_all(dq_late, "y", 0, 0, tiled=True)

    def joined(mine, came):
        return (mine.astype(f32) + came.astype(f32)).astype(bf16)

    k_far, v_far = step(dk[2], 1), step(dv[2], -1)
    v_up, k_down = step(dv[1], 1), step(dk[3], -1)
    k_up, v_down = step(joined(dk[1], k_far), 1), step(joined(dv[3], v_far), -1)
    sums = add_up((dk[0], k_up, k_down), (dv[0], v_up, v_down))
    sums = lax.all_to_all(sums, "y", 0, 0, tiled=True)

    rows, near = cap * n_grp, split * n_grp
    (dq_out,) = lay_out(
        (dq_early, dq_late), ((0, 0, near, 0, 0), (1, 0, rows - near, 0, near)), ((rows, HEADS * HEAD_DIM),))
    dk_out, dv_out = lay_out((sums,), ((0, 0, rows, 0, 0), (0, rows, rows, 1, 0)), ((rows, KV_HEADS * HEAD_DIM),) * 2)
    return tuple(array.reshape(1, rows, 1, array.shape[-1]) for array in (dq_out, dk_out, dv_out))


def solution(mesh):
    groups = mesh.shape["grp"]
    split = Mesh(mesh.devices.reshape(groups, HEADS // KV_HEADS, KV_HEADS), ("grp", "x", "y"))
    placed = P(None, "grp", ("x", "y"), None)
    out = P("grp", None, ("x", "y"), None)
    return jax.shard_map(
        on_device,
        mesh=split,
        in_specs=(placed,) * 4 + (P(),) * 3,
        out_specs=(out,) * 3,
        check_vma=False,
    )
```

```python
import functools
import math

import jax
import jax.numpy as jnp
from jax import lax
from jax.experimental import pallas as pl
from jax.experimental.pallas import tpu as pltpu
from jax.sharding import Mesh, PartitionSpec as P

HEADS = 32
KV_HEADS = 8
HEAD_DIM = 128
MAXDOC = 5
EARLY = 5
QUAD = 4
AT_ONCE = 4
NN = (((1,), (0,)), ((), ()))
NT = (((1,), (1,)), ((), ()))
TN = (((0,), (0,)), ((), ()))
f32 = jnp.float32
bf16 = jnp.bfloat16
NEG_FILL = -1e30


def dot(a, b, dims):
    return lax.dot_general(a, b, dims, preferred_element_type=f32)


def attention_kernel(begin, count, cap, early, n_x, has_carry, *refs):
    first_ref, where_ref, in_ref = refs[:3]
    near = refs[3:3 + n_x]
    if has_carry:
        far = refs[3 + n_x:3 + 2 * n_x]
        k_carry, v_carry, dq_ref = refs[3 + 2 * n_x:6 + 2 * n_x]
        refs = refs[6 + 2 * n_x:]
        dk_refs, dv_refs = refs[:n_x], refs[n_x:2 * n_x]
        refs = refs[2 * n_x:]
        queries, keys, values, s_keep, p_keep, q_acc, sem, k_acc, v_acc = refs
    else:
        dq_ref, k_acc, v_acc, queries, keys, values, s_keep, p_keep, q_acc, sem = refs[3 + n_x:]
    n_y, groups, _, head_dim = in_ref.shape
    heads = n_x
    part = groups * n_y
    span = heads * part
    rest = cap - early
    factor = 1.0 / math.sqrt(head_dim)
    power = math.log2(math.e) * factor
    my_x = where_ref[0]

    moves = []
    for slot in range(n_x):
        moves.append((near[slot].at[pl.ds(0, early)], keys.at[slot, pl.ds(0, early)]))
        moves.append((near[slot].at[pl.ds(early, early)], values.at[slot, pl.ds(0, early)]))
    if has_carry:
        for slot in range(n_x):
            moves.append((far[slot].at[pl.ds(0, rest)], keys.at[slot, pl.ds(early, rest)]))
            moves.append((far[slot].at[pl.ds(rest, rest)], values.at[slot, pl.ds(early, rest)]))
        moves.append((k_carry, k_acc.at[:, pl.ds(0, early)]))
        moves.append((v_carry, v_acc.at[:, pl.ds(0, early)]))
    copies = [pltpu.make_async_copy(source, target, sem.at[i]) for i, (source, target) in enumerate(moves)]
    for copy in copies:
        copy.start()

    per = 2 * QUAD
    mixed = groups * per
    row = lax.broadcasted_iota(jnp.int32, (mixed, mixed), 0)
    col = lax.broadcasted_iota(jnp.int32, (mixed, mixed), 1)
    turn = jnp.where((row // groups == col % per) & (row % groups == col // per), 1.0, 0.0).astype(bf16)
    quads, ones = count // QUAD, count % QUAD

    def sort_y(y, _):
        def turned(starts):
            taken = jnp.concatenate(
                [in_ref[y, :, start:start + per, :].reshape(mixed, head_dim) for start in starts], axis=1)
            out = dot(turn, taken, NN).astype(bf16)
            return [out[:, i * head_dim:(i + 1) * head_dim].reshape(per, groups, head_dim) for i in range(len(starts))]

        at = [pl.ds(pl.multiple_of(h * part + y * groups, groups), groups) for h in range(heads)]
        for j in range(quads):
            slabs = turned([(j * heads + h) * per for h in range(heads)])
            for h in range(heads):
                for kind in range(2):
                    to = kind * count + j * QUAD
                    queries[to:to + QUAD, at[h], :] = slabs[h][kind * QUAD:(kind + 1) * QUAD]
        if ones:
            slabs = turned([(quads * heads + i) * per for i in range(ones)])
            for i in range(ones):
                for h in range(heads):
                    for kind in range(2):
                        queries[kind * count + quads * QUAD + i, at[h], :] = slabs[i][2 * h + kind]
        return 0

    lax.fori_loop(0, n_y, sort_y, 0)
    for copy in copies:
        copy.wait()

    def put(block):
        at = pl.multiple_of(block * groups, groups)
        for x in range(n_x):
            dk_refs[x][:, pl.ds(at, groups), :] = (k_acc[x, block] * factor).astype(bf16).reshape(n_y, groups, head_dim)
            dv_refs[x][:, pl.ds(at, groups), :] = v_acc[x, block].astype(bf16).reshape(n_y, groups, head_dim)

    if has_carry:
        low = first_ref[begin]
        low = jnp.where(low < 0, begin, jnp.minimum(low, begin))
        lax.fori_loop(0, low, lambda block, _: (put(block), 0)[1], 0)

    key_row = lax.broadcasted_iota(jnp.int32, (part, span), 0)
    query_col = lax.broadcasted_iota(jnp.int32, (part, span), 1) % part
    key_pos = (key_row % groups) * (n_x * n_y) + key_row // groups
    query_pos = (query_col % groups) * (n_x * n_y) + query_col // groups + my_x * n_y

    def one_block(block, _):
        low = first_ref[block]
        local = block - begin
        at = pl.multiple_of(local * groups, groups)

        @pl.when(low < 0)
        def _():
            dq_ref[:, pl.ds(at, groups), :] = jnp.zeros((n_y, groups, heads * head_dim), bf16)
            zero = jnp.zeros((part, head_dim), f32)
            for x in range(n_x):
                k_acc[x, block] = zero
                v_acc[x, block] = zero
            if has_carry:
                put(block)

        @pl.when(low >= 0)
        def _():
            q = queries[local]
            g = queries[count + local]

            def score(key, stats, masked):
                high, mass, mean = stats
                slot = key - low
                top = high
                for x in range(n_x):
                    s = dot(keys[x, key], q, NT)
                    if masked:
                        x_of = lax.rem(my_x + x, n_x) * n_y
                        s = jnp.where(key_pos + x_of <= query_pos, s, NEG_FILL)
                    s_keep[slot, x] = s
                    top = jnp.maximum(top, jnp.max(s, axis=0, keepdims=True))
                shrink = jnp.exp2((high - top) * power)
                mass = mass * shrink
                mean = mean * shrink
                for x in range(n_x):
                    dp = dot(values[x, key], g, NT)
                    p_keep[slot, x] = dp
                    e = jnp.exp2((s_keep[slot, x] - top) * power)
                    mass = mass + jnp.sum(e, axis=0, keepdims=True)
                    mean = mean + jnp.sum(e * dp, axis=0, keepdims=True)
                return top, mass, mean

            none = jnp.zeros((1, span), f32)
            stats = score(block, (none + NEG_FILL, none, none), True)
            stats = lax.fori_loop(low, block, lambda key, stats: score(key, stats, False), stats)
            high, mass, mean = stats
            norm = high * power + jnp.log2(mass)
            delta = mean / mass

            def back(key, fresh):
                slot = key - low
                total = None
                for x in range(n_x):
                    p = jnp.exp2(s_keep[slot, x] * power - norm)
                    ds = (p * (p_keep[slot, x] - delta)).astype(bf16)
                    dv = dot(p.astype(bf16), g, NN)
                    dk = dot(ds, q, NN)
                    dq = dot(ds, keys[x, key], TN)
                    total = dq if total is None else total + dq
                    if fresh:
                        v_acc[x, key] = dv
                        k_acc[x, key] = dk
                    else:
                        v_acc[x, key] += dv
                        k_acc[x, key] += dk
                if fresh:
                    q_acc[...] = total
                else:
                    q_acc[...] += total

            back(block, True)
            lax.fori_loop(low, block, lambda key, _: (back(key, False), 0)[1], 0)
            for h in range(heads):
                mine = (q_acc[h * part:(h + 1) * part, :] * factor).astype(bf16)
                dq_ref[:, pl.ds(at, groups), h * head_dim:(h + 1) * head_dim] = mine.reshape(n_y, groups, head_dim)

            if has_carry:
                after = first_ref[jnp.minimum(block + 1, cap - 1)]

                @pl.when((block == cap - 1) | (after < 0) | (after > block))
                def _():
                    lax.fori_loop(low, block + 1, lambda key, _: (put(key), 0)[1], 0)
        return 0

    lax.fori_loop(begin, begin + count, one_block, 0)


def attention(first, my_x, packed, near, begin, count, late=None, carry=()):
    n_y, groups, _, head_dim = packed.shape
    n_x = HEADS // KV_HEADS
    cap = first.shape[0]
    early = near[0].shape[0] // 2
    part = groups * n_y
    span = n_x * part
    vmem = pl.BlockSpec(memory_space=pltpu.VMEM)
    smem = pl.BlockSpec(memory_space=pltpu.SMEM)
    anywhere = pl.BlockSpec(memory_space=pl.ANY)
    shape = jax.ShapeDtypeStruct
    dq = shape((n_y, count * groups, n_x * head_dim), bf16)
    has_carry = late is not None
    reach = begin + count
    slots = min(MAXDOC, reach)
    sums = (n_x, reach, part, head_dim)
    more = (*late, *carry) if has_carry else ()
    scratch = [
        pltpu.VMEM((2 * count, span, head_dim), bf16),
        pltpu.VMEM((n_x, reach, part, head_dim), bf16),
        pltpu.VMEM((n_x, reach, part, head_dim), bf16),
        pltpu.VMEM((slots, n_x, part, span), f32),
        pltpu.VMEM((slots, n_x, part, span), f32),
        pltpu.VMEM((span, head_dim), f32),
        pltpu.SemaphoreType.DMA((2 * n_x + (2 * n_x + 2 if has_carry else 0),)),
    ]
    if has_carry:
        out = (dq,) + (shape((n_y, cap * groups, head_dim), bf16),) * (2 * n_x)
        scratch = scratch + [pltpu.VMEM(sums, f32)] * 2
    else:
        out = (dq, shape(sums, f32), shape(sums, f32))
    pairs = count * 2
    return pl.pallas_call(
        functools.partial(attention_kernel, begin, count, cap, early, n_x, has_carry),
        out_shape=out,
        in_specs=[smem, smem, vmem] + [anywhere] * (len(near) + len(more)),
        out_specs=(vmem,) * len(out),
        scratch_shapes=scratch,
        compiler_params=pltpu.CompilerParams(vmem_limit_bytes=60 * 2**20),
        cost_estimate=pl.CostEstimate(
            flops=pairs * 10 * span * span * head_dim, bytes_accessed=8 * 2**20, transcendentals=pairs * 2 * span * span),
        name="attention",
    )(first, my_x, packed, *near, *more)


def pack_kernel(begin, count, cap, early, heads, *refs):
    lens_ref, groups_ref, offsets_ref, q_ref, g_ref = refs[:5]
    if early:
        k_ref, v_ref, out_ref, pick_quad, pick_one, pick_kv = refs[5:]
    else:
        out_ref, pick_quad, pick_one = refs[5:]
    _, n_grp, _, head_dim = out_ref.shape
    units = q_ref.shape[0]
    per = 2 * QUAD
    quads, ones = count // QUAD, count % QUAD

    @pl.when(pl.program_id(0) == 0)
    def _():
        lens = lens_ref[...]
        docs = lens.shape[1]
        before = lax.broadcasted_iota(jnp.int32, (docs, docs), 0) < lax.broadcasted_iota(jnp.int32, (docs, docs), 1)
        many = jnp.broadcast_to(lens, (16, docs)).astype(f32).astype(bf16)
        start = dot(many, jnp.where(before, 1.0, 0.0).astype(bf16), NN)[:1].astype(jnp.int32)
        low = groups_ref[...] * cap + offsets_ref[...]

        def choose(rows, block, shift, width):
            place = lax.broadcasted_iota(jnp.int32, (n_grp * rows, docs), 0)
            place = place // rows * cap + block(place % rows)
            inside = (place >= low) & (place < low + lens)
            source = jnp.sum(jnp.where(inside, start - low + place + 1, 0), axis=1, keepdims=True) - 1
            row = lax.broadcasted_iota(jnp.int32, (n_grp * rows, 1), 0) % rows
            wanted = jnp.where(source >= 0, source + shift(row) * units, -1)
            column = lax.broadcasted_iota(jnp.int32, (n_grp * rows, width * units), 1)
            return jnp.where(column == wanted, 1.0, 0.0).astype(bf16)

        for j in range(quads):
            pick_quad[j] = choose(per, lambda r: begin + j * QUAD + r % QUAD, lambda r: r // QUAD, 2)
        for i in range(ones):
            pick_one[i] = choose(per, lambda r: r * 0 + (begin + quads * QUAD + i), lambda r: r, 2 * heads)
        if early:
            rest = cap - early
            pick_kv[...] = choose(
                2 * cap,
                lambda r: jnp.where(r < 2 * early, r % early, early + (r - 2 * early) % rest),
                lambda r: jnp.where(r < 2 * early, r // early, (r - 2 * early) // rest),
                2)

    width = heads * head_dim
    for y in range(q_ref.shape[1] // width):
        mine = slice(y * width, (y + 1) * width)
        both = jnp.concatenate([q_ref[:, mine], g_ref[:, mine]], axis=0)
        for j in range(quads):
            moved = dot(pick_quad[j], both, NN)
            for h in range(heads):
                at = (j * heads + h) * per
                slab = moved[:, h * head_dim:(h + 1) * head_dim].reshape(n_grp, per, head_dim)
                out_ref[y, :, at:at + per, :] = slab.astype(bf16)
        if ones:
            tall = jnp.concatenate([both[:, h * head_dim:(h + 1) * head_dim] for h in range(heads)], axis=0)
        for i in range(ones):
            at = (quads * heads + i) * per
            out_ref[y, :, at:at + per, :] = dot(pick_one[i], tall, NN).reshape(n_grp, per, head_dim).astype(bf16)
        if early:
            mine = slice(y * head_dim, (y + 1) * head_dim)
            both = dot(pick_kv[...], jnp.concatenate([k_ref[:, mine], v_ref[:, mine]], axis=0), NN)
            out_ref[y, :, 2 * heads * count:, :] = both.reshape(n_grp, 2 * cap, head_dim).astype(bf16)


def pack(tables, q, g, kv, n_grp, n_y, begin, count, cap, each=AT_ONCE):
    units = q.shape[0]
    heads = q.shape[1] // (n_y * HEAD_DIM)
    rows = heads * 2 * count + (2 * cap if kv else 0)
    table = pl.BlockSpec((1, tables[0].shape[1]), lambda y: (0, 0))
    wide = pl.BlockSpec((units, each * heads * HEAD_DIM), lambda y: (0, y))
    thin = pl.BlockSpec((units, each * HEAD_DIM), lambda y: (0, y))
    tall = n_grp * 2 * QUAD
    scratch = [
        pltpu.VMEM((count // QUAD, tall, 2 * units), bf16),
        pltpu.VMEM((max(1, count % QUAD), tall, 2 * heads * units), bf16),
    ]
    if kv:
        scratch.append(pltpu.VMEM((n_grp * 2 * cap, 2 * units), bf16))
    return pl.pallas_call(
        functools.partial(pack_kernel, begin, count, cap, count if kv else 0, heads),
        out_shape=jax.ShapeDtypeStruct((n_y, n_grp, rows, HEAD_DIM), bf16),
        grid=(n_y // each,),
        in_specs=[table] * 3 + [wide] * 2 + [thin] * len(kv),
        out_specs=pl.BlockSpec((each, n_grp, rows, HEAD_DIM), lambda y: (y, 0, 0, 0)),
        scratch_shapes=scratch,
        compiler_params=pltpu.CompilerParams(vmem_limit_bytes=60 * 2**20),
        cost_estimate=pl.CostEstimate(flops=2 * 10**9, bytes_accessed=6 * 2**20, transcendentals=0),
        name="pack",
    )(*tables, q, g, *kv)


def add_kernel(*refs):
    out_ref = refs[-1]
    rows = out_ref.shape[1] // 2
    for half in range(2):
        a, b, c = refs[3 * half:3 * half + 3]
        total = a[...].astype(f32) + b[...].astype(f32) + c[...].astype(f32)
        out_ref[:, half * rows:(half + 1) * rows, :] = total.astype(bf16)


def add_up(dk_parts, dv_parts):
    n_y, rows, head_dim = dk_parts[0].shape
    vmem = pl.BlockSpec(memory_space=pltpu.VMEM)
    return pl.pallas_call(
        add_kernel,
        out_shape=jax.ShapeDtypeStruct((n_y, 2 * rows, head_dim), bf16),
        in_specs=[vmem] * 6,
        out_specs=vmem,
        compiler_params=pltpu.CompilerParams(vmem_limit_bytes=16 * 2**20),
        name="add_up",
    )(*dk_parts, *dv_parts)


def lay_kernel(pieces, *refs):
    sources = 1 + max(piece[0] for piece in pieces)
    for source, row, rows, target, at in pieces:
        taken, out_ref = refs[source], refs[sources + target]
        n_y, _, width = taken.shape
        for y in range(n_y):
            out_ref[at:at + rows, y * width:(y + 1) * width] = taken[y, row:row + rows, :]


def lay_out(arrays, pieces, shapes):
    vmem = pl.BlockSpec(memory_space=pltpu.VMEM)
    return pl.pallas_call(
        functools.partial(lay_kernel, pieces),
        out_shape=tuple(jax.ShapeDtypeStruct(shape, bf16) for shape in shapes),
        in_specs=[vmem] * len(arrays),
        out_specs=(vmem,) * len(shapes),
        compiler_params=pltpu.CompilerParams(vmem_limit_bytes=16 * 2**20),
        name="lay_out",
    )(*arrays)


def first_blocks(doc_lengths, doc_groups, doc_offsets, cap):
    place = jnp.arange(cap, dtype=jnp.int32)[:, None]
    here = (doc_groups == lax.axis_index("grp"))[None, :]
    member = here & (doc_offsets[None, :] <= place) & (place < (doc_offsets + doc_lengths)[None, :])
    return jnp.sum(jnp.where(member, doc_offsets[None, :] + 1, 0), axis=1) - 1


def step(array, by):
    n_x = lax.axis_size("x")
    return lax.ppermute(array, "x", [(i, (i + by) % n_x) for i in range(n_x)])


def on_device(q_src, k_src, v_src, grad_src, doc_lengths, doc_groups, doc_offsets):
    n_grp, n_x, n_y = lax.axis_size("grp"), lax.axis_size("x"), lax.axis_size("y")
    units = q_src.shape[0]
    docs = doc_lengths.shape[0]
    cap = docs // n_grp
    split = EARLY
    tables = tuple(table.reshape(1, docs) for table in (doc_lengths, doc_groups, doc_offsets))
    q, k, v, g = (array.reshape(units, array.shape[-1]) for array in (q_src, k_src, v_src, grad_src))

    def exchange(message):
        rows = message.shape[2]
        home = lax.all_to_all(message.reshape(n_y * n_grp, rows, HEAD_DIM), ("y", "grp"), 0, 0, tiled=True)
        return home.reshape(n_y, n_grp, rows, HEAD_DIM)

    early = exchange(pack(tables, q, g, (k, v), n_grp, n_y, 0, split, cap))
    late = exchange(pack(tables, q, g, (), n_grp, n_y, split, cap - split, cap))

    at = 2 * n_x * split

    def keys_of(first_row, rows):
        taken = early[:, :, at + first_row:at + first_row + rows]
        return taken.transpose(2, 0, 1, 3).reshape(rows, n_y * n_grp, HEAD_DIM)

    def gather(own):
        return (own, step(own, -1), step(own, 2), step(own, 1))

    near = gather(keys_of(0, 2 * split))
    far = gather(keys_of(2 * split, 2 * (cap - split)))

    first = first_blocks(doc_lengths, doc_groups, doc_offsets, cap)
    my_x = lax.axis_index("x").astype(jnp.int32).reshape(1)
    dq_early, k_sums, v_sums = attention(first, my_x, early, near, 0, split)
    dq_early, *far = lax.optimization_barrier((dq_early, *far))
    dq_late, *grads = attention(first, my_x, late, near, split, cap - split, far, (k_sums, v_sums))
    dk, dv = grads[:n_x], grads[n_x:]

    dq_early = lax.all_to_all(dq_early, "y", 0, 0, tiled=True)
    dq_late = lax.all_to_all(dq_late, "y", 0, 0, tiled=True)

    def joined(mine, came):
        return (mine.astype(f32) + came.astype(f32)).astype(bf16)

    k_far, v_far = step(dk[2], 1), step(dv[2], -1)
    v_up, k_down = step(dv[1], 1), step(dk[3], -1)
    k_up, v_down = step(joined(dk[1], k_far), 1), step(joined(dv[3], v_far), -1)
    sums = add_up((dk[0], k_up, k_down), (dv[0], v_up, v_down))
    sums = lax.all_to_all(sums, "y", 0, 0, tiled=True)

    rows, near = cap * n_grp, split * n_grp
    (dq_out,) = lay_out(
        (dq_early, dq_late), ((0, 0, near, 0, 0), (1, 0, rows - near, 0, near)), ((rows, HEADS * HEAD_DIM),))
    dk_out, dv_out = lay_out((sums,), ((0, 0, rows, 0, 0), (0, rows, rows, 1, 0)), ((rows, KV_HEADS * HEAD_DIM),) * 2)
    return tuple(array.reshape(1, rows, 1, array.shape[-1]) for array in (dq_out, dk_out, dv_out))


def solution(mesh):
    groups = mesh.shape["grp"]
    split = Mesh(mesh.devices.reshape(groups, HEADS // KV_HEADS, KV_HEADS), ("grp", "x", "y"))
    placed = P(None, "grp", ("x", "y"), None)
    out = P("grp", None, ("x", "y"), None)
    return jax.shard_map(
        on_device,
        mesh=split,
        in_specs=(placed,) * 4 + (P(),) * 3,
        out_specs=(out,) * 3,
        check_vma=False,
    )
```
